256 devices in a mesh: grp: 2 (over x_lo), gx: 16 (over z, core), gy: 8 (over y, x_hi).
Axes of the slice: x: 4 (x_hi: 2, x_lo: 2; x = x_hi * 2 + x_lo), y: 4, z: 8, core: 2. Of those that a mesh axis runs over, the one named last changes fastest.
Arguments:
- base_flow: float32 [128, 128, 256], P('gx', 'gy', 'grp'), may hold values from -4 to 4
- fields: float32 [16, 128, 128, 256], P('grp', 'gx', 'gy'), may hold values from -80 to 80, as said below
- wall_mask: int32 [128, 256], P('gy'), may hold values 0 or 1
- conduct_flag: int32 [128, 256], P('gy'), may hold values 0 or 1
Outputs:
- base_out: float32 [128, 128, 256], P('gx', 'gy', 'grp')
- ortho_fields: float32 [16, 128, 128, 256], P('grp', 'gx', 'gy')
- growth: float32 [16], replicated
The draws below stay inside these ranges and needn't reach their ends.
Inputs may be any that keep to these rules, and one draw needn't show every extreme that they name: real-valued perturbation fields.
All inputs are finite; a program needn't handle non-finite values. No bound on the sum of `wall_mask` or of `conduct_flag` on one device may be relied on, other than what follows from the above.
Results may differ from the reference program's by a relative error of at most 0.00011.
Values sent between devices are 32-bit elements; how exact they have to be, the bound alone decides.
A program may use at most 64 MiB of HBM per device.

```python
import jax
import jax.numpy as jnp
from jax import lax

NF = 16
STEPS = 2
NX = 128
NY = 128
NZ = 256


def draw_fields(key, part):
    key = jax.random.fold_in(key, 11)
    key_a, key_b, key_c = jax.random.split(key, 3)
    shape = (NF, NX, NY, NZ)
    field_scale = jnp.exp(jax.random.uniform(key_b, (NF, 1, 1, 1), jnp.float32) * jnp.log(10.0))
    row_scale = jnp.exp(jax.random.uniform(key_c, (1, NX, 1, 1), jnp.float32, jnp.log(0.5), jnp.log(2.0)))
    values = jnp.clip(jax.random.normal(key_a, shape, jnp.float32), -4.0, 4.0)
    return (values * field_scale * row_scale).astype(jnp.float32)


def with_ends(drawn, own_key, smallest, top_value):
    longest = drawn.shape.index(max(drawn.shape))
    spots = []
    for shift in (0, 1):
        where = [jax.random.randint(jax.random.fold_in(own_key, axis), (), 0, length) for axis, length in enumerate(drawn.shape)]
        where[longest] = (where[longest] + shift) % drawn.shape[longest]
        spots.append(tuple(where))
    return drawn.at[spots[0]].set(smallest).at[spots[1]].set(top_value)


def levels(key, shape, shards, least, top_value):
    loudness = 1.0
    for position, parts in shards:
        heights = jax.random.uniform(jax.random.fold_in(jax.random.fold_in(key, 6), position), (parts,), jnp.float32, least / len(shards), top_value / len(shards))
        loudness = loudness * jnp.repeat(jnp.exp(heights), shape[position] // parts).reshape((-1,) + (1,) * (len(shape) - 1 - position))
    return loudness


def scatter_about(stream_key, extent, scale, most, pieces=(), held_as=jnp.bfloat16):
    gain = levels(stream_key, extent, pieces, -0.22, 0.18) if pieces else 1.0
    result = jax.random.normal(stream_key, extent, jnp.float32) * scale * gain
    return jnp.minimum(jnp.maximum(result, -most), most).astype(held_as)


def setup_inputs(seed: int = 0) -> dict:
    streams_of = jax.random.split(jax.random.key(seed), 5)
    base_flow = scatter_about(streams_of[0], (NX, NY, NZ), 1.0, 4.0, ((0, 16), (1, 8), (2, 2)), jnp.float32)
    fields = draw_fields(jax.random.fold_in(streams_of[4], 71), 0)
    wall_mask = with_ends((jax.random.randint(streams_of[2], (NY, NZ), 0, 8) < 7).astype(jnp.int32), jax.random.fold_in(streams_of[2], 1), 0, 1)
    conduct_flag = with_ends((jax.random.randint(streams_of[3], (NY, NZ), 0, 2) < 1).astype(jnp.int32), jax.random.fold_in(streams_of[3], 1), 0, 1)
    return {"base_flow": base_flow, "fields": fields, "wall_mask": wall_mask, "conduct_flag": conduct_flag}


step_dt = 0.15
drive = 0.5

def pad_cells(a):
    a = jnp.concatenate([a[-1:], a, a[:1]], 0)
    return jnp.pad(a, ((0, 0), (1, 1), (1, 1)))

def derivs(padded):
    centre = padded[1:-1, 1:-1, 1:-1]
    beside = padded[2:, 1:-1, 1:-1] + padded[:-2, 1:-1, 1:-1]
    beside = beside + padded[1:-1, 2:, 1:-1] + padded[1:-1, :-2, 1:-1]
    beside = beside + padded[1:-1, 1:-1, 2:] + padded[1:-1, 1:-1, :-2]
    slope = (padded[2:, 1:-1, 1:-1] - padded[:-2, 1:-1, 1:-1]) * 0.5
    return (centre, beside - 6.0 * centre, slope)

def reference(base_flow, fields, wall_mask, conduct_flag):
    wall = wall_mask.astype(jnp.float32)
    damp = 0.25 * (1.0 + 3.0 * conduct_flag.astype(jnp.float32))
    base = base_flow
    for step in range(STEPS):
        centre, lap_u, dx_u = derivs(pad_cells(base))

        def advance(field):
            vc, lap_v, dx_v = derivs(pad_cells(field))
            return wall * (vc + step_dt * (lap_v - centre * dx_v - vc * dx_u - damp * vc))
        fields = lax.map(advance, fields)
        base = wall * (centre + step_dt * (lap_u - centre * dx_u - damp * centre + drive))
    flat = fields.reshape(NF, -1)
    gram = jnp.dot(flat, flat.T, precision=lax.Precision.HIGHEST) / float(NX * NY * NZ)
    lower = jnp.linalg.cholesky(gram)
    inverse = jax.scipy.linalg.solve_triangular(lower, jnp.eye(NF, dtype=jnp.float32), lower=True)
    ortho = jnp.dot(inverse, flat, precision=lax.Precision.HIGHEST).reshape(fields.shape)
    growth = jnp.log(jnp.diagonal(lower))
    return (base, ortho, growth)
```

```python
import jax
import jax.numpy as jnp
from jax import lax
from jax.experimental import pallas as pl
from jax.experimental.pallas import tpu as pltpu
from jax.sharding import PartitionSpec as P

MESH = pl.DeviceIdType.MESH
F32 = jnp.float32
GX, GY = 16, 8
LX, LY, NF, NZ = 8, 16, 8, 256
HALF = NZ // 2
CELLS = 4194304.0
P_ORDER = (4, 3, 5, 2, 6, 1, 7, 0)
Z_ORDER = (8, 7, 9, 6, 10, 5, 11, 4, 12, 3, 13, 2, 14, 1, 15)


def when(cond, fn):
    if cond is None:
        fn()
    else:
        pl.when(cond)(fn)


def remote(src, dst, send, recv, device):
    return pltpu.make_async_remote_copy(
        src_ref=src,
        dst_ref=dst,
        send_sem=send,
        recv_sem=recv,
        device_id=device,
        device_id_type=MESH,
    )


def both(*conds):
    out = None
    for c in conds:
        if c is not None:
            out = c if out is None else jnp.logical_and(out, c)
    return out


def kernel(
    base_hbm, fields_hbm, wall_ref, cond_ref,
    base_out, ortho_hbm, growth_out,
    fi, v1, w, o, ue, u1, wc, tile, al, zl, gs,
    ld_sem, out_sem, h_send, h_recv, x_send, x_recv, p_send, p_recv, z_send, z_recv,
):
    g = lax.axis_index("grp")
    gx = lax.axis_index("gx")
    gy = lax.axis_index("gy")
    other = 1 - g
    partner = (other, gx, gy)
    has_low = gy > 0
    has_high = gy < GY - 1
    lanes = pl.ds(pl.multiple_of(g * HALF, HALF), HALF)

    loads = [
        pltpu.make_async_copy(
            fields_hbm.at[f], fi.at[pl.ds(2, LX), pl.ds(2, LY), f], ld_sem.at[f]
        )
        for f in range(NF)
    ]
    loads.append(
        pltpu.make_async_copy(base_hbm, ue.at[pl.ds(2, LX), pl.ds(8, LY), lanes], ld_sem.at[NF])
    )
    for c in loads:
        c.start()

    barrier = pltpu.get_barrier_semaphore()
    count = 0
    greet = []
    for dx in (-1, 0, 1):
        for dy in (-1, 0, 1):
            for side in (0, 1):
                if dx == 0 and dy == 0 and side == 0:
                    continue
                ok = None if dy == 0 else (has_low if dy < 0 else has_high)
                who = g if side == 0 else other
                greet.append((ok, (who, lax.rem(gx + dx + GX, GX), gy + dy)))
    for y in range(GY):
        far = jnp.abs(gy - y) >= 2
        greet.append((far, (1, gx, y)))
        greet.append((both(far, g == 1), (0, gx, y)))
    for off in range(2, GX - 1):
        greet.append((g == 1, (1, lax.rem(gx + off, GX), gy)))
    for ok, dev in greet:
        when(
            ok,
            lambda dev=dev: pl.semaphore_signal(
                barrier, inc=1, device_id=dev, device_id_type=MESH
            ),
        )
        count = count + (1 if ok is None else jnp.where(ok, 1, 0))

    wc[0, pl.ds(8, LY), :] = wall_ref[...].astype(F32)
    wc[1, pl.ds(8, LY), :] = 0.1 - 0.15 * (0.25 * (1.0 + 3.0 * cond_ref[...].astype(F32)))

    for ok, row, urow, wrow in ((gy == 0, 0, 6, 7), (gy == GY - 1, LY + 2, 24, 24)):

        def clear(row=row, urow=urow, wrow=wrow):
            for x in range(LX + 4):
                fi[x, pl.ds(row, 2)] = jnp.zeros((2, NF, NZ), F32)
                ue[x, pl.ds(urow, 2), :] = jnp.zeros((2, NZ), F32)
            for i in range(2):
                wc[i, pl.ds(wrow, 1), :] = jnp.zeros((1, NZ), F32)

        pl.when(ok)(clear)

    for c in loads:
        c.wait()
    pl.semaphore_wait(barrier, count)

    halos = []

    def halo(dx, dy, src, dst, who=None):
        to = None if dy == 0 else (has_low if dy < 0 else has_high)
        frm = None if dy == 0 else (has_high if dy < 0 else has_low)
        i = len(halos)
        dev = (g if who is None else who, lax.rem(gx + dx + GX, GX), gy + dy)
        halos.append((to, frm, remote(src, dst, h_send.at[i], h_recv.at[i], dev)))

    xs, ys = pl.ds(2, LX), pl.ds(2, LY)
    yu = pl.ds(8, LY)
    for dy, src, dst in ((-1, 2, LY + 2), (1, LY, 0)):
        halo(0, dy, fi.at[xs, pl.ds(src, 2)], fi.at[xs, pl.ds(dst, 2)])
    for dx, src, dst in ((-1, 2, LX + 2), (1, LX, 0)):
        halo(dx, 0, fi.at[pl.ds(src, 2), ys], fi.at[pl.ds(dst, 2), ys])
    src = ue.at[xs, yu, lanes]
    halo(0, 0, src, src, other)
    for who in (None, other):
        for dy, s, d in ((-1, 8, 24), (1, 22, 6)):
            halo(0, dy, ue.at[xs, pl.ds(s, 2), lanes], ue.at[xs, pl.ds(d, 2), lanes], who)
        for dx, s, d in ((-1, 2, LX + 2), (1, LX, 0)):
            halo(dx, 0, ue.at[pl.ds(s, 2), yu, lanes], ue.at[pl.ds(d, 2), yu, lanes], who)
        for dx, sx, tx in ((-1, 2, LX + 2), (1, LX + 1, 1)):
            for dy, sy, ty in ((-1, 8, 24), (1, 23, 7)):
                halo(
                    dx, dy,
                    ue.at[sx, pl.ds(sy, 1), lanes], ue.at[tx, pl.ds(ty, 1), lanes], who,
                )
    for dx, sx, tx in ((-1, 2, LX + 2), (1, LX + 1, 1)):
        for dy, sy, ty in ((-1, 2, LY + 2), (1, LY + 1, 1)):
            halo(dx, dy, fi.at[sx, sy], fi.at[tx, ty])
    for dy, s, d in ((-1, 8, 24), (1, 23, 7)):
        halo(0, dy, wc.at[:, pl.ds(s, 1)], wc.at[:, pl.ds(d, 1)])

    for to, _, c in halos:
        when(to, c.start)
    u_other = pl.ds(pl.multiple_of(other * HALF, HALF), HALF)
    for i, (_, frm, c) in enumerate(halos):
        when(frm, c.wait_recv)

    lane = lax.broadcasted_iota(jnp.int32, (NF, NZ), 1)
    first = lane == 0
    last = lane == NZ - 1

    def row_step(src, su, x, y, ux, uy, wy):
        v = src[x, y]
        u = su[ux, pl.ds(uy, 1), :]
        slope = su[ux + 1, pl.ds(uy, 1), :] - su[ux - 1, pl.ds(uy, 1), :]
        near = src[x, y + 1] + src[x, y - 1]
        near = near + jnp.where(first, 0.0, pltpu.roll(v, 1, 1))
        near = near + jnp.where(last, 0.0, pltpu.roll(v, NZ - 1, 1))
        h = 0.075 * u
        out = (wc[1, pl.ds(wy, 1), :] - 0.075 * slope) * v + 0.15 * near
        out = out + (0.15 - h) * src[x + 1, y] + (0.15 + h) * src[x - 1, y]
        return wc[0, pl.ds(wy, 1), :] * out

    ulane = lax.broadcasted_iota(jnp.int32, (32, NZ), 1)

    def u_step(src, x):
        c = src[x]
        ahead, behind = src[x + 1], src[x - 1]
        near = ahead + behind + pltpu.roll(c, 1, 0) + pltpu.roll(c, 31, 0)
        near = near + jnp.where(ulane == 0, 0.0, pltpu.roll(c, 1, 1))
        near = near + jnp.where(ulane == NZ - 1, 0.0, pltpu.roll(c, NZ - 1, 1))
        return wc[0] * (
            (wc[1] - 0.075 * (ahead - behind)) * c + 0.15 * near + 0.075
        )

    @pl.loop(0, LX + 2)
    def _(x):
        u1[x] = u_step(ue, x + 1)

        @pl.loop(0, LY // 4)
        def _(b):
            for i in range(4):
                y = 1 + b * 4 + i
                v1[x, y] = row_step(fi, ue, x + 1, y + 1, x + 1, y + 7, y + 7)

    @pl.loop(1, LX + 1)
    def _(x):
        for y in (0, LY + 1):
            v1[x, y] = row_step(fi, ue, x + 1, y + 1, x + 1, y + 7, y + 7)

    def plane(x):
        @pl.loop(0, LY // 4)
        def _(b):
            for i in range(4):
                y = b * 4 + i
                w[g, x, y] = row_step(v1, u1, x + 1, y + 1, x + 1, y + 8, y + 8)

    half = LX // 2
    mine = g * half
    theirs = other * half
    sends = []
    for c in range(half):
        plane(mine + c)
        ref = w.at[g, mine + c]
        sends.append(remote(ref, ref, x_send.at[c], x_recv.at[c], partner))
        sends[-1].start()
    for c in range(half):
        plane(theirs + c)

    @pl.loop(0, LX)
    def _(x):
        c = u_step(u1, x + 1)[8:24]
        base_out[x] = jnp.where(g == 0, c[:, :HALF], c[:, HALF:])

    def rows_gram(a, b, x, acc):
        def step(y, acc):
            r = w[a, x, y]
            return tuple(acc[j] + r * w[b, x, y, pl.ds(j, 1), :] for j in range(NF))

        return lax.fori_loop(0, LY, step, acc, unroll=4)

    zeros = tuple(jnp.zeros((NF, NZ), F32) for _ in range(NF))
    own = lax.fori_loop(0, LX, lambda x, acc: rows_gram(g, g, x, acc), zeros)
    col = lax.broadcasted_iota(jnp.int32, (NF, 128), 1)
    part = jnp.zeros((NF, 128), F32)
    for j in range(NF):
        part = jnp.where(col == 8 + 8 * g + j, jnp.sum(own[j], axis=1, keepdims=True), part)
    cross = zeros
    for c in range(half):
        ref = w.at[other, theirs + c]
        remote(ref, ref, x_send.at[c], x_recv.at[c], partner).wait_recv()
        cross = rows_gram(1, 0, theirs + c, cross)
    for j in range(NF):
        part = jnp.where(col == j, jnp.sum(cross[j], axis=1, keepdims=True), part)
    me = g * GY + gy
    tile[0] = part
    al[me] = part

    def p_copy(off):
        dev = (1, gx, lax.rem(gy + off, GY))
        return remote(tile.at[0], al.at[me], p_send.at[off], p_recv.at[me], dev)

    for off in P_ORDER:
        when(g == 0 if off == 0 else None, p_copy(off).start)

    tail_ref = w.at[0, pl.ds(half, half)]
    tail = remote(tail_ref, tail_ref, x_send.at[half], x_recv.at[half], (1, gx, gy))
    final = remote(gs, gs, x_send.at[half + 1], x_recv.at[half + 1], (0, gx, gy))

    @pl.when(g == 0)
    def _():
        tail.start()
        final.wait_recv()

    def z_copy(off):
        dev = (1, lax.rem(gx + off, GX), gy)
        return remote(tile.at[1], zl.at[gx], z_send.at[off], z_recv.at[gx], dev)

    @pl.when(g == 1)
    def _():
        for s in range(2 * GY):
            c = remote(tile.at[0], al.at[s], p_send.at[0], p_recv.at[s], partner)
            when(None if s < GY else gy != s - GY, c.wait_recv)
        total = al[0]
        for s in range(1, 2 * GY):
            total = total + al[s]
        tile[1] = total
        zl[gx] = total
        for off in Z_ORDER:
            z_copy(off).start()
        for s in range(GX):
            c = remote(tile.at[1], zl.at[s], z_send.at[0], z_recv.at[s], partner)
            when(gx != s, c.wait_recv)
        total = zl[0]
        for s in range(1, GX):
            total = total + zl[s]
        gs[...] = total * (1.0 / CELLS)
        final.start()

    gram = gs[...]
    sub8 = lax.broadcasted_iota(jnp.int32, (NF, 128), 0)
    g01 = jnp.zeros((NF, 128), F32)
    for j in range(NF):
        row = jnp.where(col == sub8, gram[j : j + 1, :], 0.0)
        g01 = jnp.where(col == 8 + j, jnp.sum(row, axis=1, keepdims=True), g01)
    shifted = pltpu.roll(gram, 120, 1)
    top = jnp.where(col < 8, shifted, g01)
    low = jnp.where(col < 8, gram, shifted)
    top = jnp.where(col < 16, top, jnp.where(col == 16 + sub8, 1.0, 0.0))
    low = jnp.where(col < 16, low, jnp.where(col == 24 + sub8, 1.0, 0.0))
    m = jnp.concatenate([top, low], axis=0)
    sub = lax.broadcasted_iota(jnp.int32, (2 * NF, 128), 0)
    col16 = lax.broadcasted_iota(jnp.int32, (2 * NF, 128), 1)
    for k in range(2 * NF - 1):
        pivot = m[k : k + 1, :]
        factor = m[:, k : k + 1] / pivot[:, k : k + 1]
        m = m - jnp.where(sub > k, factor, 0.0) * pivot
    diag = jnp.where(col16 == sub, m, 0.0)
    root_row = jnp.sqrt(jnp.sum(diag, axis=0, keepdims=True))
    root_col = jnp.sqrt(jnp.sum(diag, axis=1, keepdims=True))
    growth_out[...] = jnp.log(root_row)[:, :16]
    inv = m / root_col

    def emit(groups, rows):
        cols = [
            jnp.broadcast_to(rows[:, 16 + j : 17 + j], (NF, NZ)) for j in range(NF * groups)
        ]

        def step(x, carry):
            def inner(y, carry):
                acc = None
                for b in range(groups):
                    for j in range(NF):
                        t = cols[b * NF + j] * w[b, x, y, pl.ds(j, 1), :]
                        acc = t if acc is None else acc + t
                o[x, y] = acc
                return carry

            return lax.fori_loop(0, LY, inner, carry, unroll=4)

        for part_ in range(2):
            lax.fori_loop(part_ * half, part_ * half + half, step, 0)
            for f in range(NF):
                out_copy(part_, f).start()

    def out_copy(part_, f):
        r = pl.ds(part_ * half, half)
        return pltpu.make_async_copy(
            o.at[r, :, f], ortho_hbm.at[f, r], out_sem.at[part_ * NF + f]
        )

    @pl.when(g == 0)
    def _():
        emit(1, inv[:NF])

    @pl.when(g == 1)
    def _():
        tail.wait_recv()
        emit(2, inv[NF:])

    for part_ in range(2):
        for f in range(NF):
            out_copy(part_, f).wait()
    for to, _, c in halos:
        when(to, c.wait_send)
    for c in sends:
        c.wait_send()
    for off in P_ORDER:
        when(g == 0 if off == 0 else None, p_copy(off).wait_send)

    @pl.when(g == 0)
    def _():
        tail.wait_send()

    @pl.when(g == 1)
    def _():
        final.wait_send()
        for off in Z_ORDER:
            z_copy(off).wait_send()


def body(base_flow, fields, wall_mask, conduct_flag):
    vmem = pl.BlockSpec(memory_space=pltpu.VMEM)
    hbm = pl.BlockSpec(memory_space=pl.ANY)
    dma = pltpu.SemaphoreType.DMA
    base, ortho, growth = pl.pallas_call(
        kernel,
        out_shape=[
            jax.ShapeDtypeStruct(base_flow.shape, F32),
            jax.ShapeDtypeStruct(fields.shape, F32),
            jax.ShapeDtypeStruct((1, 2 * NF), F32),
        ],
        in_specs=[hbm, hbm, vmem, vmem],
        out_specs=[vmem, hbm, vmem],
        scratch_shapes=[
            pltpu.VMEM((LX + 4, LY + 4, NF, NZ), F32),
            pltpu.VMEM((LX + 2, LY + 2, NF, NZ), F32),
            pltpu.VMEM((2, LX, LY, NF, NZ), F32),
            pltpu.VMEM((LX, LY, NF, NZ), F32),
            pltpu.VMEM((LX + 4, 32, NZ), F32),
            pltpu.VMEM((LX + 2, 32, NZ), F32),
            pltpu.VMEM((2, 32, NZ), F32),
            pltpu.VMEM((2, NF, 128), F32),
            pltpu.VMEM((2 * GY, NF, 128), F32),
            pltpu.VMEM((GX, NF, 128), F32),
            pltpu.VMEM((NF, 128), F32),
            dma((NF + 1,)),
            dma((2 * NF,)),
            dma((32,)),
            dma((32,)),
            dma((6,)),
            dma((6,)),
            dma((GY,)),
            dma((2 * GY,)),
            dma((GX,)),
            dma((GX,)),
        ],
        compiler_params=pltpu.CompilerParams(
            collective_id=0, has_side_effects=True, vmem_limit_bytes=24 << 20
        ),
    )(base_flow, fields, wall_mask, conduct_flag)
    return base, ortho, growth.reshape(2 * NF)


def solution(mesh):
    in_specs = (P("gx", "gy", "grp"), P("grp", "gx", "gy", None), P("gy", None), P("gy", None))
    out_specs = (P("gx", "gy", "grp"), P("grp", "gx", "gy", None), P())
    return jax.shard_map(body, mesh=mesh, in_specs=in_specs, out_specs=out_specs, check_vma=False)
```

```python
import jax
import jax.numpy as jnp
from jax import lax
from jax.experimental import pallas as pl
from jax.experimental.pallas import tpu as pltpu
from jax.sharding import PartitionSpec as P

MESH = pl.DeviceIdType.MESH
F32 = jnp.float32
GX, GY = 16, 8
LX, LY, NF, NZ = 8, 16, 8, 256
HALF = NZ // 2
CELLS = 4194304.0
P_ORDER = (4, 3, 5, 2, 6, 1, 7, 0)
Z_ORDER = (8, 7, 9, 6, 10, 5, 11, 4, 12, 3, 13, 2, 14, 1, 15)


def when(cond, fn):
    if cond is None:
        fn()
    else:
        pl.when(cond)(fn)


def remote(src, dst, send, recv, device):
    return pltpu.make_async_remote_copy(
        src_ref=src,
        dst_ref=dst,
        send_sem=send,
        recv_sem=recv,
        device_id=device,
        device_id_type=MESH,
    )


def both(*conds):
    out = None
    for c in conds:
        if c is not None:
            out = c if out is None else jnp.logical_and(out, c)
    return out


def kernel(
    base_hbm, fields_hbm, wall_hbm, cond_hbm,
    w, base_out, coef_out, growth_out,
    fi, v1, ue, u1, masks, wc, tile, al, zl, gs,
    ld_sem, h_send, h_recv, x_send, x_recv, p_send, p_recv, z_send, z_recv,
):
    g = lax.axis_index("grp")
    gx = lax.axis_index("gx")
    gy = lax.axis_index("gy")
    other = 1 - g
    partner = (other, gx, gy)
    has_low = gy > 0
    has_high = gy < GY - 1
    lanes = pl.ds(pl.multiple_of(g * HALF, HALF), HALF)

    loads = [
        pltpu.make_async_copy(
            base_hbm, ue.at[pl.ds(2, LX), pl.ds(8, LY), lanes], ld_sem.at[NF]
        ),
        pltpu.make_async_copy(wall_hbm, masks.at[0], ld_sem.at[NF + 1]),
        pltpu.make_async_copy(cond_hbm, masks.at[1], ld_sem.at[NF + 2]),
    ]
    loads += [
        pltpu.make_async_copy(
            fields_hbm.at[f], fi.at[pl.ds(2, LX), pl.ds(2, LY), f], ld_sem.at[f]
        )
        for f in range(NF)
    ]
    for c in loads:
        c.start()

    barrier = pltpu.get_barrier_semaphore()
    count = 0
    greet = []
    for dx in (-1, 0, 1):
        for dy in (-1, 0, 1):
            for side in (0, 1):
                if dx == 0 and dy == 0 and side == 0:
                    continue
                ok = None if dy == 0 else (has_low if dy < 0 else has_high)
                who = g if side == 0 else other
                greet.append((ok, (who, lax.rem(gx + dx + GX, GX), gy + dy)))
    for y in range(GY):
        far = jnp.abs(gy - y) >= 2
        greet.append((far, (1, gx, y)))
        greet.append((both(far, g == 1), (0, gx, y)))
    for off in range(2, GX - 1):
        greet.append((g == 1, (1, lax.rem(gx + off, GX), gy)))
    for ok, dev in greet:
        when(
            ok,
            lambda dev=dev: pl.semaphore_signal(
                barrier, inc=1, device_id=dev, device_id_type=MESH
            ),
        )
        count = count + (1 if ok is None else jnp.where(ok, 1, 0))

    for ok, row, urow, wrow in ((gy == 0, 0, 6, 7), (gy == GY - 1, LY + 2, 24, 24)):

        def clear(row=row, urow=urow, wrow=wrow):
            for x in range(LX + 4):
                fi[x, pl.ds(row, 2)] = jnp.zeros((2, NF, NZ), F32)
                ue[x, pl.ds(urow, 2), :] = jnp.zeros((2, NZ), F32)
            for i in range(2):
                wc[i, pl.ds(wrow, 1), :] = jnp.zeros((1, NZ), F32)

        pl.when(ok)(clear)

    for c in loads:
        c.wait()
    wc[0, pl.ds(8, LY), :] = masks[0].astype(F32)
    wc[1, pl.ds(8, LY), :] = 0.1 - 0.15 * (0.25 * (1.0 + 3.0 * masks[1].astype(F32)))
    pl.semaphore_wait(barrier, count)

    halos = []

    def halo(dx, dy, src, dst, who=None):
        to = None if dy == 0 else (has_low if dy < 0 else has_high)
        frm = None if dy == 0 else (has_high if dy < 0 else has_low)
        i = len(halos)
        dev = (g if who is None else who, lax.rem(gx + dx + GX, GX), gy + dy)
        halos.append((to, frm, remote(src, dst, h_send.at[i], h_recv.at[i], dev)))

    xs, ys = pl.ds(2, LX), pl.ds(2, LY)
    yu = pl.ds(8, LY)
    src = ue.at[xs, yu, lanes]
    halo(0, 0, src, src, other)
    for who in (other, None):
        for dx, sx, tx in ((-1, 2, LX + 2), (1, LX + 1, 1)):
            for dy, sy, ty in ((-1, 8, 24), (1, 23, 7)):
                halo(
                    dx, dy,
                    ue.at[sx, pl.ds(sy, 1), lanes], ue.at[tx, pl.ds(ty, 1), lanes], who,
                )
        for dy, s, d in ((-1, 8, 24), (1, 22, 6)):
            halo(0, dy, ue.at[xs, pl.ds(s, 2), lanes], ue.at[xs, pl.ds(d, 2), lanes], who)
        for dx, s, d in ((-1, 2, LX + 2), (1, LX, 0)):
            halo(dx, 0, ue.at[pl.ds(s, 2), yu, lanes], ue.at[pl.ds(d, 2), yu, lanes], who)
    for dy, s, d in ((-1, 8, 24), (1, 23, 7)):
        halo(0, dy, wc.at[:, pl.ds(s, 1)], wc.at[:, pl.ds(d, 1)])
    u_count = len(halos)
    for dx, src, dst in ((-1, 2, LX + 2), (1, LX, 0)):
        halo(dx, 0, fi.at[pl.ds(src, 2), ys], fi.at[pl.ds(dst, 2), ys])
    for dy, src, dst in ((-1, 2, LY + 2), (1, LY, 0)):
        halo(0, dy, fi.at[xs, pl.ds(src, 2)], fi.at[xs, pl.ds(dst, 2)])
    for dx, sx, tx in ((-1, 2, LX + 2), (1, LX + 1, 1)):
        for dy, sy, ty in ((-1, 2, LY + 2), (1, LY + 1, 1)):
            halo(dx, dy, fi.at[sx, sy], fi.at[tx, ty])

    for to, _, c in halos:
        when(to, c.start)

    def arrive(lo, hi):
        for _, frm, c in halos[lo:hi]:
            when(frm, c.wait_recv)

    lane = lax.broadcasted_iota(jnp.int32, (NF, NZ), 1)
    first = lane == 0
    last = lane == NZ - 1

    def row_step(src, su, x, y, ux, uy, wy):
        v = src[x, y]
        u = su[ux, pl.ds(uy, 1), :]
        slope = su[ux + 1, pl.ds(uy, 1), :] - su[ux - 1, pl.ds(uy, 1), :]
        near = src[x, y + 1] + src[x, y - 1]
        near = near + jnp.where(first, 0.0, pltpu.roll(v, 1, 1))
        near = near + jnp.where(last, 0.0, pltpu.roll(v, NZ - 1, 1))
        h = 0.075 * u
        out = (wc[1, pl.ds(wy, 1), :] - 0.075 * slope) * v + 0.15 * near
        out = out + (0.15 - h) * src[x + 1, y] + (0.15 + h) * src[x - 1, y]
        return wc[0, pl.ds(wy, 1), :] * out

    ulane = lax.broadcasted_iota(jnp.int32, (32, NZ), 1)

    def u_step(src, x):
        c = src[x]
        ahead, behind = src[x + 1], src[x - 1]
        near = ahead + behind + pltpu.roll(c, 1, 0) + pltpu.roll(c, 31, 0)
        near = near + jnp.where(ulane == 0, 0.0, pltpu.roll(c, 1, 1))
        near = near + jnp.where(ulane == NZ - 1, 0.0, pltpu.roll(c, NZ - 1, 1))
        return wc[0] * (
            (wc[1] - 0.075 * (ahead - behind)) * c + 0.15 * near + 0.075
        )

    def first_rows(x, rows):
        for y in rows:
            v1[x, y] = row_step(fi, ue, x + 1, y + 1, x + 1, y + 7, y + 7)

    def second_rows(x, rows):
        for y in rows:
            w[g, x, y] = row_step(v1, u1, x + 1, y + 1, x + 1, y + 8, y + 8)

    def first_inner(x):
        @pl.loop(0, 2)
        def _(b):
            first_rows(x, [2 + b * 7 + i for i in range(7)])

    def second_inner(x):
        @pl.loop(0, 2)
        def _(b):
            second_rows(x, [2 + b * 6 + i for i in range(6)])

    half = LX // 2
    inner = pl.ds(2, LY - 4)
    edges = (pl.ds(0, 2), pl.ds(LY - 2, 2))

    def pieces(s):
        near = [w.at[s, 2 + 2 * s + i, inner] for i in range(2)]
        far = [w.at[s, 6 * s + i, inner] for i in range(2)]
        rim = [w.at[s, pl.ds(half * s, half), e] for e in edges]
        return near + far + rim

    sends = [
        remote(r, r, x_send.at[i], x_recv.at[i], partner) for i, r in enumerate(pieces(g))
    ]
    gets = [
        remote(r, r, x_send.at[i], x_recv.at[i], partner)
        for i, r in enumerate(pieces(other))
    ]

    arrive(0, u_count)

    @pl.loop(0, LX + 2)
    def _(x):
        u1[x] = u_step(ue, x + 1)

    @pl.loop(0, 4)
    def _(i):
        first_inner(2 + 2 * g + i)

    for i in range(2):
        second_inner(2 + 2 * g + i)
        sends[i].start()

    arrive(u_count, u_count + 2)
    for i in range(2):
        first_inner(8 * g + i)
    for i in range(2):
        second_inner(6 * g + i)
        sends[2 + i].start()

    @pl.loop(0, 4)
    def _(i):
        first_inner(6 * other + i)

    arrive(u_count + 2, len(halos))

    @pl.loop(0, LX + 2)
    def _(x):
        first_rows(x, (1, LY))

    @pl.loop(1, LX + 1)
    def _(x):
        first_rows(x, (0, LY + 1))

    for e in range(2):

        @pl.loop(0, half)
        def _(x, e=e):
            second_rows(half * g + x, (0, 1) if e == 0 else (LY - 2, LY - 1))

        sends[4 + e].start()

    @pl.loop(0, half)
    def _(x):
        second_inner(half * other + x)
        second_rows(half * other + x, (0, 1, LY - 2, LY - 1))

    @pl.loop(0, LX)
    def _(x):
        c = u_step(u1, x + 1)[8:24]
        base_out[x] = jnp.where(g == 0, c[:, :HALF], c[:, HALF:])

    def gram_rows(a, b, x, lo, n, acc, unroll):
        def step(y, acc):
            r = w[a, x, y]
            return tuple(acc[j] + r * w[b, x, y, pl.ds(j, 1), :] for j in range(NF))

        return lax.fori_loop(lo, lo + n, step, acc, unroll=unroll)

    zeros = tuple(jnp.zeros((NF, NZ), F32) for _ in range(NF))
    own = lax.fori_loop(0, LX, lambda x, acc: gram_rows(g, g, x, 0, LY, acc, 4), zeros)
    col = lax.broadcasted_iota(jnp.int32, (NF, 128), 1)
    part = jnp.zeros((NF, 128), F32)
    for j in range(NF):
        part = jnp.where(col == 8 + 8 * g + j, jnp.sum(own[j], axis=1, keepdims=True), part)
    cross = zeros
    for i in range(4):
        gets[i].wait_recv()
        x = (2 + 2 * other if i < 2 else 6 * other) + i % 2
        cross = gram_rows(1, 0, x, 2, LY - 4, cross, 4)
    for e in range(2):
        gets[4 + e].wait_recv()
        cross = lax.fori_loop(
            0, half,
            lambda x, acc: gram_rows(1, 0, half * other + x, e * (LY - 2), 2, acc, 2),
            cross,
        )
    for j in range(NF):
        part = jnp.where(col == j, jnp.sum(cross[j], axis=1, keepdims=True), part)
    me = g * GY + gy
    tile[0] = part
    al[me] = part

    def p_copy(off):
        dev = (1, gx, lax.rem(gy + off, GY))
        return remote(tile.at[0], al.at[me], p_send.at[off], p_recv.at[me], dev)

    for off in P_ORDER:
        when(g == 0 if off == 0 else None, p_copy(off).start)

    tail_ref = w.at[0, pl.ds(half, half)]
    tail = remote(tail_ref, tail_ref, x_send.at[6], x_recv.at[6], (1, gx, gy))
    final = remote(gs, gs, x_send.at[7], x_recv.at[7], (0, gx, gy))

    @pl.when(g == 0)
    def _():
        tail.start()
        final.wait_recv()

    def z_copy(off):
        dev = (1, lax.rem(gx + off, GX), gy)
        return remote(tile.at[1], zl.at[gx], z_send.at[off], z_recv.at[gx], dev)

    @pl.when(g == 1)
    def _():
        for s in range(2 * GY):
            c = remote(tile.at[0], al.at[s], p_send.at[0], p_recv.at[s], partner)
            when(None if s < GY else gy != s - GY, c.wait_recv)
        total = al[0]
        for s in range(1, 2 * GY):
            total = total + al[s]
        tile[1] = total
        zl[gx] = total
        for off in Z_ORDER:
            z_copy(off).start()
        for s in range(GX):
            c = remote(tile.at[1], zl.at[s], z_send.at[0], z_recv.at[s], partner)
            when(gx != s, c.wait_recv)
        total = zl[0]
        for s in range(1, GX):
            total = total + zl[s]
        gs[...] = total * (1.0 / CELLS)
        final.start()

    gram = gs[...]
    sub8 = lax.broadcasted_iota(jnp.int32, (NF, 128), 0)
    g01 = jnp.zeros((NF, 128), F32)
    for j in range(NF):
        row = jnp.where(col == sub8, gram[j : j + 1, :], 0.0)
        g01 = jnp.where(col == 8 + j, jnp.sum(row, axis=1, keepdims=True), g01)
    shifted = pltpu.roll(gram, 120, 1)
    top = jnp.where(col < 8, shifted, g01)
    low = jnp.where(col < 8, gram, shifted)
    top = jnp.where(col < 16, top, jnp.where(col == 16 + sub8, 1.0, 0.0))
    low = jnp.where(col < 16, low, jnp.where(col == 24 + sub8, 1.0, 0.0))
    m = jnp.concatenate([top, low], axis=0)
    sub = lax.broadcasted_iota(jnp.int32, (2 * NF, 128), 0)
    col16 = lax.broadcasted_iota(jnp.int32, (2 * NF, 128), 1)
    for k in range(2 * NF - 1):
        pivot = m[k : k + 1, :]
        factor = m[:, k : k + 1] / pivot[:, k : k + 1]
        m = m - jnp.where(sub > k, factor, 0.0) * pivot
    diag = jnp.where(col16 == sub, m, 0.0)
    root_row = jnp.sqrt(jnp.sum(diag, axis=0, keepdims=True))
    root_col = jnp.sqrt(jnp.sum(diag, axis=1, keepdims=True))
    growth_out[...] = jnp.log(root_row)[:, :16]
    inv = m / root_col
    coef_out[...] = jnp.where(g == 0, inv[:NF], inv[NF:])

    @pl.when(g == 1)
    def _():
        tail.wait_recv()

    for to, _, c in halos:
        when(to, c.wait_send)
    for c in sends:
        c.wait_send()
    for off in P_ORDER:
        when(g == 0 if off == 0 else None, p_copy(off).wait_send)

    @pl.when(g == 0)
    def _():
        tail.wait_send()

    @pl.when(g == 1)
    def _():
        final.wait_send()
        for off in Z_ORDER:
            z_copy(off).wait_send()


def apply_kernel(
    w, base, coef, growth, base_hbm, ortho_hbm, growth_hbm, o, out_sem
):
    g = lax.axis_index("grp")
    small = [
        pltpu.make_async_copy(base, base_hbm, out_sem.at[4 * NF]),
        pltpu.make_async_copy(growth, growth_hbm, out_sem.at[4 * NF + 1]),
    ]
    for c in small:
        c.start()
    step = LX // 4

    def out_copy(q, f):
        r = pl.ds(q * step, step)
        return pltpu.make_async_copy(
            o.at[r, :, f], ortho_hbm.at[f, r], out_sem.at[q * NF + f]
        )

    def emit(groups):
        cols = [
            jnp.broadcast_to(coef[:, 16 + j : 17 + j], (NF, NZ)) for j in range(NF * groups)
        ]

        def plane(x, carry):
            def row(y, carry):
                acc = None
                for b in range(groups):
                    for j in range(NF):
                        t = cols[b * NF + j] * w[b, x, y, pl.ds(j, 1), :]
                        acc = t if acc is None else acc + t
                o[x, y] = acc
                return carry

            return lax.fori_loop(0, LY, row, carry, unroll=4)

        for q in range(4):
            lax.fori_loop(q * step, (q + 1) * step, plane, 0)
            for f in range(NF):
                out_copy(q, f).start()

    @pl.when(g == 0)
    def _():
        emit(1)

    @pl.when(g == 1)
    def _():
        emit(2)

    for q in range(4):
        for f in range(NF):
            out_copy(q, f).wait()
    for c in small:
        c.wait()


def body(*arrays):
    base_flow, fields = arrays[:2]
    vmem = pl.BlockSpec(memory_space=pltpu.VMEM)
    hbm = pl.BlockSpec(memory_space=pltpu.HBM)
    dma = pltpu.SemaphoreType.DMA
    stepped, base, coef, growth = pl.pallas_call(
        kernel,
        out_shape=[
            pltpu.VMEM((2, LX, LY, NF, NZ), F32),
            pltpu.VMEM(base_flow.shape, F32),
            pltpu.VMEM((NF, 128), F32),
            pltpu.VMEM((1, 2 * NF), F32),
        ],
        in_specs=[hbm] * 4,
        out_specs=[vmem] * 4,
        scratch_shapes=[
            pltpu.VMEM((LX + 4, LY + 4, NF, NZ), F32),
            pltpu.VMEM((LX + 2, LY + 2, NF, NZ), F32),
            pltpu.VMEM((LX + 4, 32, NZ), F32),
            pltpu.VMEM((LX + 2, 32, NZ), F32),
            pltpu.VMEM((2, LY, NZ), jnp.int32),
            pltpu.VMEM((2, 32, NZ), F32),
            pltpu.VMEM((2, NF, 128), F32),
            pltpu.VMEM((2 * GY, NF, 128), F32),
            pltpu.VMEM((GX, NF, 128), F32),
            pltpu.VMEM((NF, 128), F32),
            dma((NF + 3,)),
            dma((32,)),
            dma((32,)),
            dma((8,)),
            dma((8,)),
            dma((GY,)),
            dma((2 * GY,)),
            dma((GX,)),
            dma((GX,)),
        ],
        compiler_params=pltpu.CompilerParams(
            collective_id=0, has_side_effects=True, vmem_limit_bytes=16 << 20
        ),
    )(*(pltpu.with_memory_space_constraint(a, pltpu.HBM) for a in arrays))
    base, ortho, growth = pl.pallas_call(
        apply_kernel,
        out_shape=[
            jax.ShapeDtypeStruct(base_flow.shape, F32),
            jax.ShapeDtypeStruct(fields.shape, F32),
            jax.ShapeDtypeStruct((1, 2 * NF), F32),
        ],
        in_specs=[vmem] * 4,
        out_specs=[hbm] * 3,
        scratch_shapes=[pltpu.VMEM((LX, LY, NF, NZ), F32), dma((4 * NF + 2,))],
        compiler_params=pltpu.CompilerParams(vmem_limit_bytes=16 << 20),
    )(stepped, base, coef, growth)
    return base, ortho, growth.reshape(2 * NF)


def solution(mesh):
    in_specs = (P("gx", "gy", "grp"), P("grp", "gx", "gy", None), P("gy", None), P("gy", None))
    out_specs = (P("gx", "gy", "grp"), P("grp", "gx", "gy", None), P())
    return jax.shard_map(body, mesh=mesh, in_specs=in_specs, out_specs=out_specs, check_vma=False)
```

```python
import jax
import jax.numpy as jnp
from jax import lax
from jax.experimental import pallas as pl
from jax.experimental.pallas import tpu as pltpu
from jax.sharding import PartitionSpec as P

MESH = pl.DeviceIdType.MESH
F32 = jnp.float32
GX, GY = 16, 8
LX, LY, NF, NZ = 8, 16, 8, 256
HALF = NZ // 2
PARTS = 2
CELLS = 4194304.0
P_ORDER = tuple((off, swap) for off in (4, 3, 5, 2, 6, 1, 7, 0) for swap in (1, 0) if off or swap)
TAIL = ((4, 2), (6, 2))
Z_ORDER = (8, 7, 9, 6, 10, 5, 11, 4, 12, 3, 13, 2, 14, 1, 15)


def when(cond, fn):
    if cond is None:
        fn()
    else:
        pl.when(cond)(fn)


def remote(src, dst, send, recv, device):
    return pltpu.make_async_remote_copy(
        src_ref=src,
        dst_ref=dst,
        send_sem=send,
        recv_sem=recv,
        device_id=device,
        device_id_type=MESH,
    )


def kernel(
    base_hbm, fields_hbm, wall_hbm, cond_hbm,
    w, base_out, coef_out, growth_out,
    fi, v1, ue, u1, masks, wc, tile, al, zl,
    ld_sem, h_send, h_recv, x_send, x_recv, p_send, p_recv, z_send, z_recv,
):
    g = lax.axis_index("grp")
    gx = lax.axis_index("gx")
    gy = lax.axis_index("gy")
    other = 1 - g
    partner = (other, gx, gy)
    has_low = gy > 0
    has_high = gy < GY - 1
    lanes = pl.ds(pl.multiple_of(g * HALF, HALF), HALF)

    barrier = pltpu.get_barrier_semaphore()
    count = 0
    greet = []
    for dy in (-1, 1, 0):
        for dx in (0, -1, 1):
            for side in (0, 1):
                if dx == 0 and dy == 0 and side == 0:
                    continue
                ok = None if dy == 0 else (has_low if dy < 0 else has_high)
                who = g if side == 0 else other
                greet.append((ok, (who, lax.rem(gx + dx + GX, GX), gy + dy)))
    def signal(ok, dev):
        when(
            ok,
            lambda: pl.semaphore_signal(barrier, inc=1, device_id=dev, device_id_type=MESH),
        )

    for ok, dev in greet:
        signal(ok, dev)
    close = len(greet)

    loads = [
        pltpu.make_async_copy(
            base_hbm, ue.at[pl.ds(2, LX), pl.ds(8, LY), lanes], ld_sem.at[NF]
        ),
        pltpu.make_async_copy(wall_hbm, masks.at[0], ld_sem.at[NF + 1]),
        pltpu.make_async_copy(cond_hbm, masks.at[1], ld_sem.at[NF + 2]),
    ]
    loads += [
        pltpu.make_async_copy(
            fields_hbm.at[f], fi.at[pl.ds(2, LX), pl.ds(2, LY), f], ld_sem.at[f]
        )
        for f in range(NF)
    ]
    for c in loads:
        c.start()

    for y in range(GY):
        far = jnp.abs(gy - y) >= 2
        greet.append((far, (g, gx, y)))
        greet.append((far, (other, gx, y)))
    for off in range(2, GX - 1):
        greet.append((None, (g, lax.rem(gx + off, GX), gy)))
    for ok, dev in greet[close:]:
        signal(ok, dev)
    for ok, _ in greet:
        count = count + (1 if ok is None else jnp.where(ok, 1, 0))

    for ok, row, urow, wrow in ((gy == 0, 0, 6, 7), (gy == GY - 1, LY + 2, 24, 24)):

        def clear(row=row, urow=urow, wrow=wrow):
            for x in range(LX + 4):
                fi[x, pl.ds(row, 2)] = jnp.zeros((2, NF, NZ), F32)
                ue[x, pl.ds(urow, 2), :] = jnp.zeros((2, NZ), F32)
            for i in range(2):
                wc[i, pl.ds(wrow, 1), :] = jnp.zeros((1, NZ), F32)

        pl.when(ok)(clear)

    for c in loads[:3]:
        c.wait()
    wc[0, pl.ds(8, LY), :] = masks[0].astype(F32)
    wc[1, pl.ds(8, LY), :] = 0.1 - 0.15 * (0.25 * (1.0 + 3.0 * masks[1].astype(F32)))
    pl.semaphore_wait(barrier, count)

    halos = []

    def halo(dx, dy, src, dst, who=None):
        to = None if dy == 0 else (has_low if dy < 0 else has_high)
        frm = None if dy == 0 else (has_high if dy < 0 else has_low)
        i = len(halos)
        dev = (g if who is None else who, lax.rem(gx + dx + GX, GX), gy + dy)
        halos.append((to, frm, remote(src, dst, h_send.at[i], h_recv.at[i], dev)))

    xs, ys = pl.ds(2, LX), pl.ds(2, LY)
    yu = pl.ds(8, LY)
    src = ue.at[xs, yu, lanes]
    halo(0, 0, src, src, other)
    for who in (other, None):
        for dx, sx, tx in ((-1, 2, LX + 2), (1, LX + 1, 1)):
            for dy, sy, ty in ((-1, 8, 24), (1, 23, 7)):
                halo(
                    dx, dy,
                    ue.at[sx, pl.ds(sy, 1), lanes], ue.at[tx, pl.ds(ty, 1), lanes], who,
                )
        for dy, s, d in ((-1, 8, 24), (1, 22, 6)):
            halo(0, dy, ue.at[xs, pl.ds(s, 2), lanes], ue.at[xs, pl.ds(d, 2), lanes], who)
    for dx, s, d in ((-1, 2, LX + 2), (1, LX, 0)):
        halo(dx, 0, ue.at[pl.ds(s, 2), yu, lanes], ue.at[pl.ds(d, 2), yu, lanes])
    for dy, s, d in ((-1, 8, 24), (1, 23, 7)):
        halo(0, dy, wc.at[:, pl.ds(s, 1)], wc.at[:, pl.ds(d, 1)])
    u_count = len(halos)
    for dx, src, dst in ((-1, 2, LX + 2), (1, LX, 0)):
        halo(dx, 0, fi.at[pl.ds(src, 2), ys], fi.at[pl.ds(dst, 2), ys])
    for dy, src, dst in ((-1, 2, LY + 2), (1, LY, 0)):
        halo(0, dy, fi.at[xs, pl.ds(src, 2)], fi.at[xs, pl.ds(dst, 2)])
    for dx, sx, tx in ((-1, 2, LX + 2), (1, LX + 1, 1)):
        for dy, sy, ty in ((-1, 2, LY + 2), (1, LY + 1, 1)):
            halo(dx, dy, fi.at[sx, sy], fi.at[tx, ty])
    first_count = len(halos)
    lanes2 = pl.ds(pl.multiple_of(other * HALF, HALF), HALF)
    for dx, s, d in ((-1, 2, LX + 2), (1, LX, 0)):
        halo(dx, 0, ue.at[pl.ds(s, 2), yu, lanes2], ue.at[pl.ds(d, 2), yu, lanes2])

    for to, _, c in halos[:u_count]:
        when(to, c.start)
    for c in loads[3:]:
        c.wait()
    for to, _, c in halos[u_count:first_count]:
        when(to, c.start)

    def arrive(lo, hi):
        for _, frm, c in halos[lo:hi]:
            when(frm, c.wait_recv)

    lane = lax.broadcasted_iota(jnp.int32, (NF, NZ), 1)
    first = lane == 0
    last = lane == NZ - 1

    def row_step(src, su, x, y, ux, uy, wy):
        v = src[x, y]
        u = su[ux, pl.ds(uy, 1), :]
        slope = su[ux + 1, pl.ds(uy, 1), :] - su[ux - 1, pl.ds(uy, 1), :]
        near = src[x, y + 1] + src[x, y - 1]
        near = near + jnp.where(first, 0.0, pltpu.roll(v, 1, 1))
        near = near + jnp.where(last, 0.0, pltpu.roll(v, NZ - 1, 1))
        h = 0.075 * u
        out = (wc[1, pl.ds(wy, 1), :] - 0.075 * slope) * v + 0.15 * near
        out = out + (0.15 - h) * src[x + 1, y] + (0.15 + h) * src[x - 1, y]
        return wc[0, pl.ds(wy, 1), :] * out

    ulane = lax.broadcasted_iota(jnp.int32, (32, NZ), 1)

    def u_step(src, x):
        c = src[x]
        ahead, behind = src[x + 1], src[x - 1]
        near = ahead + behind + pltpu.roll(c, 1, 0) + pltpu.roll(c, 31, 0)
        near = near + jnp.where(ulane == 0, 0.0, pltpu.roll(c, 1, 1))
        near = near + jnp.where(ulane == NZ - 1, 0.0, pltpu.roll(c, NZ - 1, 1))
        return wc[0] * (
            (wc[1] - 0.075 * (ahead - behind)) * c + 0.15 * near + 0.075
        )

    def first_rows(x, rows):
        for y in rows:
            v1[x, y] = row_step(fi, ue, x + 1, y + 1, x + 1, y + 7, y + 7)

    def second_rows(x, rows):
        for y in rows:
            w[g, x, y] = row_step(v1, u1, x + 1, y + 1, x + 1, y + 8, y + 8)

    half = LX // 2
    inner = pl.ds(2, LY - 4)
    edges = (pl.ds(0, 2), pl.ds(LY - 2, 2))

    def plane_of(k, group):
        near = jnp.where(k < 2, 2 + k, 3 - k)
        x = jnp.where(k < 4, near, k)
        return jnp.where(group == 0, x, LX - 1 - x)

    def plane_ref(i, group):
        return w.at[group, plane_of(i, group), inner]

    def plane_send(i):
        r = plane_ref(i, g)
        return remote(r, r, x_send.at[i], x_recv.at[i], partner)

    def rim_send(e, group):
        r = w.at[group, pl.ds(half * group, half), edges[e]]
        return remote(r, r, x_send.at[4 + e], x_recv.at[4 + e], partner)

    arrive(0, 1)
    for _, _, c in halos[first_count:]:
        c.start()

    @pl.loop(0, LX + 2)
    def _(k):
        @pl.when(k == 1)
        def _():
            arrive(1, u_count)
            arrive(first_count, len(halos))

            @pl.loop(0, (LX + 2) // 2)
            def _(x):
                for i in range(2):
                    u1[2 * x + i] = u_step(ue, 2 * x + i + 1)

        @pl.when(k == 4)
        def _():
            arrive(u_count, u_count + 2)

        x = jnp.where(k < 4, 2 + k, jnp.where(k < 6, 5 - k, k))
        first_rows(jnp.where(g == 0, x, LX + 1 - x), range(2, LY))

        @pl.when(k >= 2)
        def _():
            second_rows(plane_of(k - 2, g), range(2, LY - 2))

        @pl.when(jnp.logical_and(k >= 2, k < 6))
        def _():
            plane_send(k - 2).start()

    arrive(u_count + 2, first_count)

    @pl.loop(0, (LX + 2) // 2)
    def _(x):
        for i in range(2):
            first_rows(2 * x + i, (0, 1, LY, LY + 1))

    @pl.loop(0, half)
    def _(h):
        for i in range(2):
            x = 2 * h + i
            x = jnp.where(g == 0, x, LX - 1 - x)
            second_rows(x, (0, 1, LY - 2, LY - 1))

        @pl.when(h == 1)
        def _():
            for e in range(2):
                rim_send(e, g).start()

    @pl.loop(0, LX // 2)
    def _(x):
        for i in range(2):
            c = u_step(u1, 2 * x + i + 1)[8:24]
            base_out[2 * x + i] = jnp.where(g == 0, c[:, :HALF], c[:, HALF:])

    def gram_rows(a, b, x, lo, n, acc, unroll):
        def step(y, acc):
            r = w[a, x, y]
            return tuple(acc[j] + r * w[b, x, y, pl.ds(j, 1), :] for j in range(NF))

        return lax.fori_loop(lo, lo + n, step, acc, unroll=unroll)

    zeros = tuple(jnp.zeros((NF, NZ), F32) for _ in range(NF))
    own = lax.fori_loop(0, LX, lambda x, acc: gram_rows(g, g, x, 0, LY, acc, 4), zeros)
    col = lax.broadcasted_iota(jnp.int32, (NF, 128), 1)
    part = jnp.zeros((NF, 128), F32)
    for j in range(NF):
        part = jnp.where(col == 8 + 8 * g + j, jnp.sum(own[j], axis=1, keepdims=True), part)
    cross = zeros
    for i in range(4):
        plane_send(i).wait_recv()
        cross = gram_rows(1, 0, plane_of(i, other), 2, LY - 4, cross, 4)
    for e in range(2):
        rim_send(e, other).wait_recv()

    def rim_gram(x, acc):
        acc = gram_rows(1, 0, half * other + x, 0, 2, acc, 2)
        return gram_rows(1, 0, half * other + x, LY - 2, 2, acc, 2)

    cross = lax.fori_loop(0, half, rim_gram, cross)
    for j in range(NF):
        part = jnp.where(col == j, jnp.sum(cross[j], axis=1, keepdims=True), part)
    me = g * GY + gy
    sub8 = lax.broadcasted_iota(jnp.int32, (NF, 128), 0)
    quarter = sub8 & 3
    wide = jnp.where(quarter == 0, part, 0.0)
    for k in range(1, 4):
        wide = jnp.where(quarter == k, pltpu.roll(part, 32 * k, 1), wide)
    part = jnp.concatenate(
        [jnp.sum(wide[4 * r : 4 * r + 4], axis=0, keepdims=True) for r in range(2)], axis=0
    )
    tile[0] = part
    al[me] = part

    def p_copy(i):
        off, swap = P_ORDER[i]
        dev = (other if swap else g, gx, lax.rem(gy + off, GY))
        return remote(tile.at[0], al.at[me], p_send.at[i], p_recv.at[me], dev)

    for i in range(len(P_ORDER)):
        p_copy(i).start()

    def tail(i):
        lo, n = TAIL[i]
        r = w.at[0, pl.ds(lo, n)]
        return remote(r, r, x_send.at[6 + i], x_recv.at[6 + i], (1, gx, gy))

    def tail_start(i):
        @pl.when(g == 0)
        def _():
            tail(i).start()

    def z_copy(off):
        dev = (g, lax.rem(gx + off, GX), gy)
        return remote(tile.at[1], zl.at[gx], z_send.at[off], z_recv.at[gx], dev)

    tail_start(0)
    for s in range(2 * GY):
        c = remote(tile.at[0], al.at[s], p_send.at[0], p_recv.at[s], partner)
        when(me != s, c.wait_recv)
    total = al[0]
    for s in range(1, 2 * GY):
        total = total + al[s]
    tile[1] = total
    zl[gx] = total
    for off in Z_ORDER:
        z_copy(off).start()
    tail_start(1)
    for s in range(GX):
        c = remote(tile.at[1], zl.at[s], z_send.at[0], z_recv.at[s], partner)
        when(gx != s, c.wait_recv)
    total = zl[0]
    for s in range(1, GX):
        total = total + zl[s]

    total = total * (1.0 / CELLS)
    wide = jnp.where(sub8 < 4, total[0:1], total[1:2])
    gram = wide
    for k in range(1, 4):
        gram = jnp.where(quarter == k, pltpu.roll(wide, 128 - 32 * k, 1), gram)
    g01 = jnp.zeros((NF, 128), F32)
    for j in range(NF):
        row = jnp.where(col == sub8, gram[j : j + 1, :], 0.0)
        g01 = jnp.where(col == 8 + j, jnp.sum(row, axis=1, keepdims=True), g01)
    shifted = pltpu.roll(gram, 120, 1)
    top = jnp.where(col < 8, shifted, g01)
    low = jnp.where(col < 8, gram, shifted)
    top = jnp.where(col < 16, top, jnp.where(col == 16 + sub8, 1.0, 0.0))
    low = jnp.where(col < 16, low, jnp.where(col == 24 + sub8, 1.0, 0.0))
    m = jnp.concatenate([top, low], axis=0)
    sub = lax.broadcasted_iota(jnp.int32, (2 * NF, 128), 0)
    col16 = lax.broadcasted_iota(jnp.int32, (2 * NF, 128), 1)
    for k in range(2 * NF - 1):
        pivot = m[k : k + 1, :]
        factor = m[:, k : k + 1] / pivot[:, k : k + 1]
        m = m - jnp.where(sub > k, factor, 0.0) * pivot
    diag = jnp.where(col16 == sub, m, 0.0)
    root_row = jnp.sqrt(jnp.sum(diag, axis=0, keepdims=True))
    root_col = jnp.sqrt(jnp.sum(diag, axis=1, keepdims=True))
    growth_out[...] = jnp.log(root_row)[:, :16]
    inv = m / root_col
    coef_out[...] = jnp.where(g == 0, inv[:NF], inv[NF:])

    @pl.when(g == 1)
    def _():
        for i in range(2):
            tail(i).wait_recv()

    for to, _, c in halos:
        when(to, c.wait_send)
    for i in range(4):
        plane_send(i).wait_send()
    for e in range(2):
        rim_send(e, g).wait_send()
    for i in range(len(P_ORDER)):
        p_copy(i).wait_send()
    for off in Z_ORDER:
        z_copy(off).wait_send()

    @pl.when(g == 0)
    def _():
        for i in range(2):
            tail(i).wait_send()


def apply_kernel(
    w, base, coef, growth, base_hbm, ortho_hbm, growth_hbm, o, out_sem
):
    g = lax.axis_index("grp")
    small = [
        pltpu.make_async_copy(base, base_hbm, out_sem.at[PARTS * NF]),
        pltpu.make_async_copy(growth, growth_hbm, out_sem.at[PARTS * NF + 1]),
    ]
    for c in small:
        c.start()
    step = LX // PARTS

    def out_copy(q, f):
        r = pl.ds(q * step, step)
        return pltpu.make_async_copy(
            o.at[r, :, f], ortho_hbm.at[f, r], out_sem.at[q * NF + f]
        )

    def emit(groups):
        cols = [
            jnp.broadcast_to(coef[:, 16 + j : 17 + j], (NF, NZ)) for j in range(NF * groups)
        ]

        def plane(x, carry):
            def row(y, carry):
                acc = None
                for b in range(groups):
                    for j in range(NF):
                        t = cols[b * NF + j] * w[b, x, y, pl.ds(j, 1), :]
                        acc = t if acc is None else acc + t
                o[x, y] = acc
                return carry

            return lax.fori_loop(0, LY, row, carry, unroll=4)

        for q in range(PARTS):
            lax.fori_loop(q * step, (q + 1) * step, plane, 0)
            for f in range(NF):
                out_copy(q, f).start()

    @pl.when(g == 0)
    def _():
        emit(1)

    @pl.when(g == 1)
    def _():
        emit(2)

    for q in range(PARTS):
        for f in range(NF):
            out_copy(q, f).wait()
    for c in small:
        c.wait()


def body(*arrays):
    base_flow, fields = arrays[:2]
    vmem = pl.BlockSpec(memory_space=pltpu.VMEM)
    hbm = pl.BlockSpec(memory_space=pltpu.HBM)
    dma = pltpu.SemaphoreType.DMA
    stepped, base, coef, growth = pl.pallas_call(
        kernel,
        out_shape=[
            pltpu.VMEM((2, LX, LY, NF, NZ), F32),
            pltpu.VMEM(base_flow.shape, F32),
            pltpu.VMEM((NF, 128), F32),
            pltpu.VMEM((1, 2 * NF), F32),
        ],
        in_specs=[hbm] * 4,
        out_specs=[vmem] * 4,
        scratch_shapes=[
            pltpu.VMEM((LX + 4, LY + 4, NF, NZ), F32),
            pltpu.VMEM((LX + 2, LY + 2, NF, NZ), F32),
            pltpu.VMEM((LX + 4, 32, NZ), F32),
            pltpu.VMEM((LX + 2, 32, NZ), F32),
            pltpu.VMEM((2, LY, NZ), jnp.int32),
            pltpu.VMEM((2, 32, NZ), F32),
            pltpu.VMEM((2, 2, 128), F32),
            pltpu.VMEM((2 * GY, 2, 128), F32),
            pltpu.VMEM((GX, 2, 128), F32),
            dma((NF + 3,)),
            dma((32,)),
            dma((32,)),
            dma((8,)),
            dma((8,)),
            dma((2 * GY,)),
            dma((2 * GY,)),
            dma((GX,)),
            dma((GX,)),
        ],
        compiler_params=pltpu.CompilerParams(
            collective_id=0, has_side_effects=True, vmem_limit_bytes=16 << 20
        ),
    )(*(pltpu.with_memory_space_constraint(a, pltpu.HBM) for a in arrays))
    base, ortho, growth = pl.pallas_call(
        apply_kernel,
        out_shape=[
            jax.ShapeDtypeStruct(base_flow.shape, F32),
            jax.ShapeDtypeStruct(fields.shape, F32),
            jax.ShapeDtypeStruct((1, 2 * NF), F32),
        ],
        in_specs=[vmem] * 4,
        out_specs=[hbm] * 3,
        scratch_shapes=[pltpu.VMEM((LX, LY, NF, NZ), F32), dma((PARTS * NF + 2,))],
        compiler_params=pltpu.CompilerParams(vmem_limit_bytes=16 << 20),
    )(stepped, base, coef, growth)
    return base, ortho, growth.reshape(2 * NF)


def solution(mesh):
    in_specs = (P("gx", "gy", "grp"), P("grp", "gx", "gy", None), P("gy", None), P("gy", None))
    out_specs = (P("gx", "gy", "grp"), P("grp", "gx", "gy", None), P())
    return jax.shard_map(body, mesh=mesh, in_specs=in_specs, out_specs=out_specs, check_vma=False)
```

```python
import jax
import jax.numpy as jnp
from jax import lax
from jax.experimental import pallas as pl
from jax.experimental.pallas import tpu as pltpu
from jax.sharding import PartitionSpec as P

MESH = pl.DeviceIdType.MESH
F32 = jnp.float32
GX, GY = 16, 8
LX, LY, NF, NZ = 8, 16, 8, 256
HALF = NZ // 2
PARTS = 2
CELLS = 4194304.0
P_ORDER = tuple((off, swap) for off in (4, 3, 5, 2, 6, 1, 7, 0) for swap in (1, 0) if off or swap)
TAIL = ((4, 1), (5, 2), (7, 1))
Z_ORDER = (8, 7, 9, 6, 10, 5, 11, 4, 12, 3, 13, 2, 14, 1, 15)


def when(cond, fn):
    if cond is None:
        fn()
    else:
        pl.when(cond)(fn)


def remote(src, dst, send, recv, device):
    return pltpu.make_async_remote_copy(
        src_ref=src,
        dst_ref=dst,
        send_sem=send,
        recv_sem=recv,
        device_id=device,
        device_id_type=MESH,
    )


def kernel(
    base_hbm, fields_hbm, wall_hbm, cond_hbm,
    w, base_out, coef_out, growth_out,
    fi, v1, ue, u1, masks, wc, tile, al, zl,
    ld_sem, h_send, h_recv, x_send, x_recv, p_send, p_recv, z_send, z_recv,
):
    g = lax.axis_index("grp")
    gx = lax.axis_index("gx")
    gy = lax.axis_index("gy")
    other = 1 - g
    partner = (other, gx, gy)
    has_low = gy > 0
    has_high = gy < GY - 1
    lanes = pl.ds(pl.multiple_of(g * HALF, HALF), HALF)

    barrier = pltpu.get_barrier_semaphore()
    count = 0
    greet = []
    for dy in (-1, 1, 0):
        for dx in (0, -1, 1):
            for side in (0, 1):
                if dx == 0 and dy == 0 and side == 0:
                    continue
                ok = None if dy == 0 else (has_low if dy < 0 else has_high)
                who = g if side == 0 else other
                greet.append((ok, (who, lax.rem(gx + dx + GX, GX), gy + dy)))
    def signal(ok, dev):
        when(
            ok,
            lambda: pl.semaphore_signal(barrier, inc=1, device_id=dev, device_id_type=MESH),
        )

    for ok, dev in greet:
        signal(ok, dev)
    close = len(greet)

    loads = [
        pltpu.make_async_copy(
            base_hbm, ue.at[pl.ds(2, LX), pl.ds(8, LY), lanes], ld_sem.at[NF]
        ),
        pltpu.make_async_copy(wall_hbm, masks.at[0], ld_sem.at[NF + 1]),
        pltpu.make_async_copy(cond_hbm, masks.at[1], ld_sem.at[NF + 2]),
    ]
    loads += [
        pltpu.make_async_copy(
            fields_hbm.at[f], fi.at[pl.ds(2, LX), pl.ds(2, LY), f], ld_sem.at[f]
        )
        for f in range(NF)
    ]
    for c in loads:
        c.start()

    for y in range(GY):
        far = jnp.abs(gy - y) >= 2
        greet.append((far, (g, gx, y)))
        greet.append((far, (other, gx, y)))
    for off in range(2, GX - 1):
        greet.append((None, (g, lax.rem(gx + off, GX), gy)))
    for ok, dev in greet[close:]:
        signal(ok, dev)
    for ok, _ in greet:
        count = count + (1 if ok is None else jnp.where(ok, 1, 0))

    for ok, row, urow, wrow in ((gy == 0, 0, 6, 7), (gy == GY - 1, LY + 2, 24, 24)):

        def clear(row=row, urow=urow, wrow=wrow):
            for x in range(LX + 4):
                fi[x, pl.ds(row, 2)] = jnp.zeros((2, NF, NZ), F32)
                ue[x, pl.ds(urow, 2), :] = jnp.zeros((2, NZ), F32)
            for i in range(2):
                wc[i, pl.ds(wrow, 1), :] = jnp.zeros((1, NZ), F32)

        pl.when(ok)(clear)

    for c in loads[:3]:
        c.wait()
    wc[0, pl.ds(8, LY), :] = masks[0].astype(F32)
    wc[1, pl.ds(8, LY), :] = 0.1 - 0.15 * (0.25 * (1.0 + 3.0 * masks[1].astype(F32)))
    pl.semaphore_wait(barrier, count)

    halos = []

    def halo(dx, dy, src, dst, who=None):
        to = None if dy == 0 else (has_low if dy < 0 else has_high)
        frm = None if dy == 0 else (has_high if dy < 0 else has_low)
        i = len(halos)
        dev = (g if who is None else who, lax.rem(gx + dx + GX, GX), gy + dy)
        halos.append((to, frm, remote(src, dst, h_send.at[i], h_recv.at[i], dev)))

    xs, ys = pl.ds(2, LX), pl.ds(2, LY)
    yu = pl.ds(8, LY)
    src = ue.at[xs, yu, lanes]
    halo(0, 0, src, src, other)
    for who in (other, None):
        for dx, sx, tx in ((-1, 2, LX + 2), (1, LX + 1, 1)):
            for dy, sy, ty in ((-1, 8, 24), (1, 23, 7)):
                halo(
                    dx, dy,
                    ue.at[sx, pl.ds(sy, 1), lanes], ue.at[tx, pl.ds(ty, 1), lanes], who,
                )
        for dy, s, d in ((-1, 8, 24), (1, 22, 6)):
            halo(0, dy, ue.at[xs, pl.ds(s, 2), lanes], ue.at[xs, pl.ds(d, 2), lanes], who)
    for dx, s, d in ((-1, 2, LX + 2), (1, LX, 0)):
        halo(dx, 0, ue.at[pl.ds(s, 2), yu, lanes], ue.at[pl.ds(d, 2), yu, lanes])
    for dy, s, d in ((-1, 8, 24), (1, 23, 7)):
        halo(0, dy, wc.at[:, pl.ds(s, 1)], wc.at[:, pl.ds(d, 1)])
    u_count = len(halos)
    for dx, src, dst in ((-1, 2, LX + 2), (1, LX, 0)):
        halo(dx, 0, fi.at[pl.ds(src, 2), ys], fi.at[pl.ds(dst, 2), ys])
    for dy, src, dst in ((-1, 2, LY + 2), (1, LY, 0)):
        halo(0, dy, fi.at[xs, pl.ds(src, 2)], fi.at[xs, pl.ds(dst, 2)])
    for dx, sx, tx in ((-1, 2, LX + 2), (1, LX + 1, 1)):
        for dy, sy, ty in ((-1, 2, LY + 2), (1, LY + 1, 1)):
            halo(dx, dy, fi.at[sx, sy], fi.at[tx, ty])
    first_count = len(halos)
    lanes2 = pl.ds(pl.multiple_of(other * HALF, HALF), HALF)
    for dx, s, d in ((-1, 2, LX + 2), (1, LX, 0)):
        halo(dx, 0, ue.at[pl.ds(s, 2), yu, lanes2], ue.at[pl.ds(d, 2), yu, lanes2])

    for to, _, c in halos[:u_count]:
        when(to, c.start)
    for c in loads[3:]:
        c.wait()
    for to, _, c in halos[u_count:first_count]:
        when(to, c.start)

    def arrive(lo, hi):
        for _, frm, c in halos[lo:hi]:
            when(frm, c.wait_recv)

    lane = lax.broadcasted_iota(jnp.int32, (NF, NZ), 1)
    first = lane == 0
    last = lane == NZ - 1

    def row_step(src, su, x, y, ux, uy, wy):
        v = src[x, y]
        u = su[ux, pl.ds(uy, 1), :]
        slope = su[ux + 1, pl.ds(uy, 1), :] - su[ux - 1, pl.ds(uy, 1), :]
        near = src[x, y + 1] + src[x, y - 1]
        near = near + jnp.where(first, 0.0, pltpu.roll(v, 1, 1))
        near = near + jnp.where(last, 0.0, pltpu.roll(v, NZ - 1, 1))
        h = 0.075 * u
        out = (wc[1, pl.ds(wy, 1), :] - 0.075 * slope) * v + 0.15 * near
        out = out + (0.15 - h) * src[x + 1, y] + (0.15 + h) * src[x - 1, y]
        return wc[0, pl.ds(wy, 1), :] * out

    ulane = lax.broadcasted_iota(jnp.int32, (32, NZ), 1)

    def u_step(src, x):
        c = src[x]
        ahead, behind = src[x + 1], src[x - 1]
        near = ahead + behind + pltpu.roll(c, 1, 0) + pltpu.roll(c, 31, 0)
        near = near + jnp.where(ulane == 0, 0.0, pltpu.roll(c, 1, 1))
        near = near + jnp.where(ulane == NZ - 1, 0.0, pltpu.roll(c, NZ - 1, 1))
        return wc[0] * (
            (wc[1] - 0.075 * (ahead - behind)) * c + 0.15 * near + 0.075
        )

    def first_rows(x, rows):
        for y in rows:
            v1[x, y] = row_step(fi, ue, x + 1, y + 1, x + 1, y + 7, y + 7)

    def second_rows(x, rows):
        for y in rows:
            w[g, x, y] = row_step(v1, u1, x + 1, y + 1, x + 1, y + 8, y + 8)

    half = LX // 2
    inner = pl.ds(2, LY - 4)
    edges = (pl.ds(0, 2), pl.ds(LY - 2, 2))

    def plane_of(k, group):
        near = jnp.where(k < 2, 2 + k, 3 - k)
        x = jnp.where(k < 4, near, k)
        return jnp.where(group == 0, x, LX - 1 - x)

    def plane_ref(i, group):
        return w.at[group, plane_of(i, group), inner]

    def plane_send(i):
        r = plane_ref(i, g)
        return remote(r, r, x_send.at[i], x_recv.at[i], partner)

    def rim_send(e, group):
        r = w.at[group, pl.ds(half * group, half), edges[e]]
        return remote(r, r, x_send.at[4 + e], x_recv.at[4 + e], partner)

    arrive(0, 1)
    for _, _, c in halos[first_count:]:
        c.start()

    @pl.loop(0, LX + 2)
    def _(k):
        @pl.when(k == 1)
        def _():
            arrive(1, u_count)
            arrive(first_count, len(halos))

            @pl.loop(0, (LX + 2) // 2)
            def _(x):
                for i in range(2):
                    u1[2 * x + i] = u_step(ue, 2 * x + i + 1)

        @pl.when(k == 4)
        def _():
            arrive(u_count, u_count + 2)

        x = jnp.where(k < 4, 2 + k, jnp.where(k < 6, 5 - k, k))
        first_rows(jnp.where(g == 0, x, LX + 1 - x), range(2, LY))

        @pl.when(k >= 2)
        def _():
            second_rows(plane_of(k - 2, g), range(2, LY - 2))

        @pl.when(jnp.logical_and(k >= 2, k < 6))
        def _():
            plane_send(k - 2).start()

    arrive(u_count + 2, first_count)

    @pl.loop(0, (LX + 2) // 2)
    def _(x):
        for i in range(2):
            first_rows(2 * x + i, (0, 1, LY, LY + 1))

    @pl.loop(0, half)
    def _(h):
        for i in range(2):
            x = 2 * h + i
            x = jnp.where(g == 0, x, LX - 1 - x)
            second_rows(x, (0, 1, LY - 2, LY - 1))

        @pl.when(h == 1)
        def _():
            for e in range(2):
                rim_send(e, g).start()

    def tail(i):
        lo, n = TAIL[i]
        r = w.at[0, pl.ds(lo, n)]
        return remote(r, r, x_send.at[6 + i], x_recv.at[6 + i], (1, gx, gy))

    def tail_start(i):
        @pl.when(g == 0)
        def _():
            tail(i).start()

    tail_start(0)

    @pl.loop(0, LX // 2)
    def _(x):
        for i in range(2):
            c = u_step(u1, 2 * x + i + 1)[8:24]
            base_out[2 * x + i] = jnp.where(g == 0, c[:, :HALF], c[:, HALF:])

    def gram_rows(a, b, x, lo, n, acc, unroll):
        def step(y, acc):
            r = w[a, x, y]
            return tuple(acc[j] + r * w[b, x, y, pl.ds(j, 1), :] for j in range(NF))

        return lax.fori_loop(lo, lo + n, step, acc, unroll=unroll)

    zeros = tuple(jnp.zeros((NF, NZ), F32) for _ in range(NF))
    own = lax.fori_loop(0, LX, lambda x, acc: gram_rows(g, g, x, 0, LY, acc, 4), zeros)
    col = lax.broadcasted_iota(jnp.int32, (NF, 128), 1)
    part = jnp.zeros((NF, 128), F32)
    for j in range(NF):
        part = jnp.where(col == 8 + 8 * g + j, jnp.sum(own[j], axis=1, keepdims=True), part)
    cross = zeros
    for i in range(4):
        plane_send(i).wait_recv()
        cross = gram_rows(1, 0, plane_of(i, other), 2, LY - 4, cross, 4)
    for e in range(2):
        rim_send(e, other).wait_recv()

    def rim_gram(x, acc):
        acc = gram_rows(1, 0, half * other + x, 0, 2, acc, 2)
        return gram_rows(1, 0, half * other + x, LY - 2, 2, acc, 2)

    cross = lax.fori_loop(0, half, rim_gram, cross)
    for j in range(NF):
        part = jnp.where(col == j, jnp.sum(cross[j], axis=1, keepdims=True), part)
    me = g * GY + gy
    sub8 = lax.broadcasted_iota(jnp.int32, (NF, 128), 0)
    quarter = sub8 & 3
    wide = jnp.where(quarter == 0, part, 0.0)
    for k in range(1, 4):
        wide = jnp.where(quarter == k, pltpu.roll(part, 32 * k, 1), wide)
    part = jnp.concatenate(
        [jnp.sum(wide[4 * r : 4 * r + 4], axis=0, keepdims=True) for r in range(2)], axis=0
    )
    tile[0] = part
    al[me] = part

    def p_copy(i):
        off, swap = P_ORDER[i]
        dev = (other if swap else g, gx, lax.rem(gy + off, GY))
        return remote(tile.at[0], al.at[me], p_send.at[i], p_recv.at[me], dev)

    for i in range(len(P_ORDER)):
        p_copy(i).start()

    def z_copy(off):
        dev = (g, lax.rem(gx + off, GX), gy)
        return remote(tile.at[1], zl.at[gx], z_send.at[off], z_recv.at[gx], dev)

    tail_start(1)
    for s in range(2 * GY):
        c = remote(tile.at[0], al.at[s], p_send.at[0], p_recv.at[s], partner)
        when(me != s, c.wait_recv)
    total = al[0]
    for s in range(1, 2 * GY):
        total = total + al[s]
    tile[1] = total
    zl[gx] = total
    for off in Z_ORDER:
        z_copy(off).start()
    tail_start(2)
    for s in range(GX):
        c = remote(tile.at[1], zl.at[s], z_send.at[0], z_recv.at[s], partner)
        when(gx != s, c.wait_recv)
    total = zl[0]
    for s in range(1, GX):
        total = total + zl[s]

    total = total * (1.0 / CELLS)
    wide = jnp.where(sub8 < 4, total[0:1], total[1:2])
    gram = wide
    for k in range(1, 4):
        gram = jnp.where(quarter == k, pltpu.roll(wide, 128 - 32 * k, 1), gram)
    g01 = jnp.zeros((NF, 128), F32)
    for j in range(NF):
        row = jnp.where(col == sub8, gram[j : j + 1, :], 0.0)
        g01 = jnp.where(col == 8 + j, jnp.sum(row, axis=1, keepdims=True), g01)
    shifted = pltpu.roll(gram, 120, 1)
    top = jnp.where(col < 8, shifted, g01)
    low = jnp.where(col < 8, gram, shifted)
    top = jnp.where(col < 16, top, jnp.where(col == 16 + sub8, 1.0, 0.0))
    low = jnp.where(col < 16, low, jnp.where(col == 24 + sub8, 1.0, 0.0))
    m = jnp.concatenate([top, low], axis=0)
    sub = lax.broadcasted_iota(jnp.int32, (2 * NF, 128), 0)
    col16 = lax.broadcasted_iota(jnp.int32, (2 * NF, 128), 1)
    spread = [jnp.broadcast_to(m[:, j : j + 1], m.shape) for j in range(2 * NF)]
    for k in range(2 * NF - 1):
        factor = jnp.where(sub > k, spread[k] / spread[k][k : k + 1, :], 0.0)
        for j in range(k + 1, 2 * NF):
            spread[j] = spread[j] - factor * spread[j][k : k + 1, :]
        m = m - factor * m[k : k + 1, :]
    diag = jnp.where(col16 == sub, m, 0.0)
    root_row = jnp.sqrt(jnp.sum(diag, axis=0, keepdims=True))
    root_col = jnp.sqrt(jnp.sum(diag, axis=1, keepdims=True))
    growth_out[...] = jnp.log(root_row)[:, :16]
    inv = m / root_col
    coef_out[...] = jnp.where(g == 0, inv[:NF], inv[NF:])

    @pl.when(g == 1)
    def _():
        for i in range(len(TAIL)):
            tail(i).wait_recv()

    for to, _, c in halos:
        when(to, c.wait_send)
    for i in range(4):
        plane_send(i).wait_send()
    for e in range(2):
        rim_send(e, g).wait_send()
    for i in range(len(P_ORDER)):
        p_copy(i).wait_send()
    for off in Z_ORDER:
        z_copy(off).wait_send()

    @pl.when(g == 0)
    def _():
        for i in range(len(TAIL)):
            tail(i).wait_send()


def apply_kernel(
    w, base, coef, growth, base_hbm, ortho_hbm, growth_hbm, o, out_sem
):
    g = lax.axis_index("grp")
    small = [
        pltpu.make_async_copy(base, base_hbm, out_sem.at[PARTS * NF]),
        pltpu.make_async_copy(growth, growth_hbm, out_sem.at[PARTS * NF + 1]),
    ]
    for c in small:
        c.start()
    step = LX // PARTS

    def out_copy(q, f):
        r = pl.ds(q * step, step)
        return pltpu.make_async_copy(
            o.at[r, :, f], ortho_hbm.at[f, r], out_sem.at[q * NF + f]
        )

    def emit(groups):
        cols = [
            jnp.broadcast_to(coef[:, 16 + j : 17 + j], (NF, NZ)) for j in range(NF * groups)
        ]

        def plane(x, carry):
            def row(y, carry):
                acc = None
                for b in range(groups):
                    for j in range(NF):
                        t = cols[b * NF + j] * w[b, x, y, pl.ds(j, 1), :]
                        acc = t if acc is None else acc + t
                o[x, y] = acc
                return carry

            return lax.fori_loop(0, LY, row, carry, unroll=8)

        for q in range(PARTS):
            lax.fori_loop(q * step, (q + 1) * step, plane, 0)
            for f in range(NF):
                out_copy(q, f).start()

    @pl.when(g == 0)
    def _():
        emit(1)

    @pl.when(g == 1)
    def _():
        emit(2)

    for q in range(PARTS):
        for f in range(NF):
            out_copy(q, f).wait()
    for c in small:
        c.wait()


def body(*arrays):
    base_flow, fields = arrays[:2]
    vmem = pl.BlockSpec(memory_space=pltpu.VMEM)
    hbm = pl.BlockSpec(memory_space=pltpu.HBM)
    dma = pltpu.SemaphoreType.DMA
    stepped, base, coef, growth = pl.pallas_call(
        kernel,
        out_shape=[
            pltpu.VMEM((2, LX, LY, NF, NZ), F32),
            pltpu.VMEM(base_flow.shape, F32),
            pltpu.VMEM((NF, 128), F32),
            pltpu.VMEM((1, 2 * NF), F32),
        ],
        in_specs=[hbm] * 4,
        out_specs=[vmem] * 4,
        scratch_shapes=[
            pltpu.VMEM((LX + 4, LY + 4, NF, NZ), F32),
            pltpu.VMEM((LX + 2, LY + 2, NF, NZ), F32),
            pltpu.VMEM((LX + 4, 32, NZ), F32),
            pltpu.VMEM((LX + 2, 32, NZ), F32),
            pltpu.VMEM((2, LY, NZ), jnp.int32),
            pltpu.VMEM((2, 32, NZ), F32),
            pltpu.VMEM((2, 2, 128), F32),
            pltpu.VMEM((2 * GY, 2, 128), F32),
            pltpu.VMEM((GX, 2, 128), F32),
            dma((NF + 3,)),
            dma((32,)),
            dma((32,)),
            dma((9,)),
            dma((9,)),
            dma((2 * GY,)),
            dma((2 * GY,)),
            dma((GX,)),
            dma((GX,)),
        ],
        compiler_params=pltpu.CompilerParams(
            collective_id=0, has_side_effects=True, vmem_limit_bytes=16 << 20
        ),
    )(*(pltpu.with_memory_space_constraint(a, pltpu.HBM) for a in arrays))
    base, ortho, growth = pl.pallas_call(
        apply_kernel,
        out_shape=[
            jax.ShapeDtypeStruct(base_flow.shape, F32),
            jax.ShapeDtypeStruct(fields.shape, F32),
            jax.ShapeDtypeStruct((1, 2 * NF), F32),
        ],
        in_specs=[vmem] * 4,
        out_specs=[hbm] * 3,
        scratch_shapes=[pltpu.VMEM((LX, LY, NF, NZ), F32), dma((PARTS * NF + 2,))],
        compiler_params=pltpu.CompilerParams(vmem_limit_bytes=16 << 20),
    )(stepped, base, coef, growth)
    return base, ortho, growth.reshape(2 * NF)


def solution(mesh):
    in_specs = (P("gx", "gy", "grp"), P("grp", "gx", "gy", None), P("gy", None), P("gy", None))
    out_specs = (P("gx", "gy", "grp"), P("grp", "gx", "gy", None), P())
    return jax.shard_map(body, mesh=mesh, in_specs=in_specs, out_specs=out_specs, check_vma=False)
```

```python
import jax
import jax.numpy as jnp
from jax import lax
from jax.experimental import pallas as pl
from jax.experimental.pallas import tpu as pltpu
from jax.sharding import PartitionSpec as P

MESH = pl.DeviceIdType.MESH
F32 = jnp.float32
GX, GY = 16, 8
LX, LY, NF, NZ = 8, 16, 8, 256
HALF = NZ // 2
PARTS = 2
CELLS = 4194304.0
P_ORDER = tuple((off, swap) for off in (4, 3, 5, 2, 6, 1, 7, 0) for swap in (1, 0) if off or swap)
TAIL = ((4, 1), (5, 2), (7, 1))
Z_ORDER = (8, 7, 9, 6, 10, 5, 11, 4, 12, 3, 13, 2, 14, 1, 15)


def when(cond, fn):
    if cond is None:
        fn()
    else:
        pl.when(cond)(fn)


def remote(src, dst, send, recv, device):
    return pltpu.make_async_remote_copy(
        src_ref=src,
        dst_ref=dst,
        send_sem=send,
        recv_sem=recv,
        device_id=device,
        device_id_type=MESH,
    )


def kernel(
    base_hbm, fields_hbm, wall_hbm, cond_hbm,
    w, base_out, coef_out, growth_out,
    fi, v1, ue, u1, masks, wc, tile, al, zl,
    ld_sem, h_send, h_recv, x_send, x_recv, p_send, p_recv, z_send, z_recv,
):
    g = lax.axis_index("grp")
    gx = lax.axis_index("gx")
    gy = lax.axis_index("gy")
    other = 1 - g
    partner = (other, gx, gy)
    has_low = gy > 0
    has_high = gy < GY - 1
    lanes = pl.ds(pl.multiple_of(g * HALF, HALF), HALF)

    barrier = pltpu.get_barrier_semaphore()
    count = 0
    greet = []
    for dy in (-1, 1, 0):
        for dx in (0, -1, 1):
            for side in (0, 1):
                if dx == 0 and dy == 0 and side == 0:
                    continue
                ok = None if dy == 0 else (has_low if dy < 0 else has_high)
                who = g if side == 0 else other
                greet.append((ok, (who, lax.rem(gx + dx + GX, GX), gy + dy)))
    def signal(ok, dev):
        when(
            ok,
            lambda: pl.semaphore_signal(barrier, inc=1, device_id=dev, device_id_type=MESH),
        )

    for ok, dev in greet:
        signal(ok, dev)
    close = len(greet)

    loads = [
        pltpu.make_async_copy(
            base_hbm, ue.at[pl.ds(2, LX), pl.ds(8, LY), lanes], ld_sem.at[NF]
        ),
        pltpu.make_async_copy(wall_hbm, masks.at[0], ld_sem.at[NF + 1]),
        pltpu.make_async_copy(cond_hbm, masks.at[1], ld_sem.at[NF + 2]),
    ]
    loads += [
        pltpu.make_async_copy(
            fields_hbm.at[f], fi.at[pl.ds(2, LX), pl.ds(2, LY), f], ld_sem.at[f]
        )
        for f in range(NF)
    ]
    for c in loads:
        c.start()

    for y in range(GY):
        far = jnp.abs(gy - y) >= 2
        greet.append((far, (g, gx, y)))
        greet.append((far, (other, gx, y)))
    for off in range(2, GX - 1):
        greet.append((None, (g, lax.rem(gx + off, GX), gy)))
    for ok, dev in greet[close:]:
        signal(ok, dev)
    for ok, _ in greet:
        count = count + (1 if ok is None else jnp.where(ok, 1, 0))

    for ok, row, urow, wrow in ((gy == 0, 0, 6, 7), (gy == GY - 1, LY + 2, 24, 24)):

        def clear(row=row, urow=urow, wrow=wrow):
            for x in range(LX + 4):
                fi[x, pl.ds(row, 2)] = jnp.zeros((2, NF, NZ), F32)
                ue[x, pl.ds(urow, 2), :] = jnp.zeros((2, NZ), F32)
            for i in range(2):
                wc[i, pl.ds(wrow, 1), :] = jnp.zeros((1, NZ), F32)

        pl.when(ok)(clear)

    for c in loads[:3]:
        c.wait()
    wc[0, pl.ds(8, LY), :] = masks[0].astype(F32)
    wc[1, pl.ds(8, LY), :] = 0.1 - 0.15 * (0.25 * (1.0 + 3.0 * masks[1].astype(F32)))
    pl.semaphore_wait(barrier, count)

    halos = []

    def halo(dx, dy, src, dst, who=None):
        to = None if dy == 0 else (has_low if dy < 0 else has_high)
        frm = None if dy == 0 else (has_high if dy < 0 else has_low)
        i = len(halos)
        dev = (g if who is None else who, lax.rem(gx + dx + GX, GX), gy + dy)
        halos.append((to, frm, remote(src, dst, h_send.at[i], h_recv.at[i], dev)))

    xs, ys = pl.ds(2, LX), pl.ds(2, LY)
    yu = pl.ds(8, LY)
    src = ue.at[xs, yu, lanes]
    halo(0, 0, src, src, other)
    for who in (other, None):
        for dx, sx, tx in ((-1, 2, LX + 2), (1, LX + 1, 1)):
            for dy, sy, ty in ((-1, 8, 24), (1, 23, 7)):
                halo(
                    dx, dy,
                    ue.at[sx, pl.ds(sy, 1), lanes], ue.at[tx, pl.ds(ty, 1), lanes], who,
                )
        for dy, s, d in ((-1, 8, 24), (1, 22, 6)):
            halo(0, dy, ue.at[xs, pl.ds(s, 2), lanes], ue.at[xs, pl.ds(d, 2), lanes], who)
    for dx, s, d in ((-1, 2, LX + 2), (1, LX, 0)):
        halo(dx, 0, ue.at[pl.ds(s, 2), yu, lanes], ue.at[pl.ds(d, 2), yu, lanes])
    for dy, s, d in ((-1, 8, 24), (1, 23, 7)):
        halo(0, dy, wc.at[:, pl.ds(s, 1)], wc.at[:, pl.ds(d, 1)])
    u_count = len(halos)
    for dx, src, dst in ((-1, 2, LX + 2), (1, LX, 0)):
        halo(dx, 0, fi.at[pl.ds(src, 2), ys], fi.at[pl.ds(dst, 2), ys])
    for dy, src, dst in ((-1, 2, LY + 2), (1, LY, 0)):
        halo(0, dy, fi.at[xs, pl.ds(src, 2)], fi.at[xs, pl.ds(dst, 2)])
    for dx, sx, tx in ((-1, 2, LX + 2), (1, LX + 1, 1)):
        for dy, sy, ty in ((-1, 2, LY + 2), (1, LY + 1, 1)):
            halo(dx, dy, fi.at[sx, sy], fi.at[tx, ty])
    first_count = len(halos)
    lanes2 = pl.ds(pl.multiple_of(other * HALF, HALF), HALF)
    for dx, s, d in ((-1, 2, LX + 2), (1, LX, 0)):
        halo(dx, 0, ue.at[pl.ds(s, 2), yu, lanes2], ue.at[pl.ds(d, 2), yu, lanes2])

    for to, _, c in halos[:u_count]:
        when(to, c.start)
    for c in loads[3:]:
        c.wait()
    for to, _, c in halos[u_count:first_count]:
        when(to, c.start)

    def arrive(lo, hi):
        for _, frm, c in halos[lo:hi]:
            when(frm, c.wait_recv)

    lane = lax.broadcasted_iota(jnp.int32, (NF, NZ), 1)
    first = lane == 0
    last = lane == NZ - 1

    def row_step(src, su, x, y, ux, uy, wy):
        v = src[x, y]
        u = su[ux, pl.ds(uy, 1), :]
        slope = su[ux + 1, pl.ds(uy, 1), :] - su[ux - 1, pl.ds(uy, 1), :]
        near = src[x, y + 1] + src[x, y - 1]
        near = near + jnp.where(first, 0.0, pltpu.roll(v, 1, 1))
        near = near + jnp.where(last, 0.0, pltpu.roll(v, NZ - 1, 1))
        h = 0.075 * u
        out = (wc[1, pl.ds(wy, 1), :] - 0.075 * slope) * v + 0.15 * near
        out = out + (0.15 - h) * src[x + 1, y] + (0.15 + h) * src[x - 1, y]
        return wc[0, pl.ds(wy, 1), :] * out

    ulane = lax.broadcasted_iota(jnp.int32, (32, NZ), 1)

    def u_step(src, x):
        c = src[x]
        ahead, behind = src[x + 1], src[x - 1]
        near = ahead + behind + pltpu.roll(c, 1, 0) + pltpu.roll(c, 31, 0)
        near = near + jnp.where(ulane == 0, 0.0, pltpu.roll(c, 1, 1))
        near = near + jnp.where(ulane == NZ - 1, 0.0, pltpu.roll(c, NZ - 1, 1))
        return wc[0] * (
            (wc[1] - 0.075 * (ahead - behind)) * c + 0.15 * near + 0.075
        )

    def first_rows(x, rows):
        for y in rows:
            v1[x, y] = row_step(fi, ue, x + 1, y + 1, x + 1, y + 7, y + 7)

    def second_rows(x, rows):
        for y in rows:
            w[g, x, y] = row_step(v1, u1, x + 1, y + 1, x + 1, y + 8, y + 8)

    half = LX // 2
    inner = pl.ds(2, LY - 4)
    edges = (pl.ds(0, 2), pl.ds(LY - 2, 2))

    def plane_of(k, group):
        near = jnp.where(k < 2, 2 + k, 3 - k)
        x = jnp.where(k < 4, near, k)
        return jnp.where(group == 0, x, LX - 1 - x)

    def plane_ref(i, group):
        return w.at[group, plane_of(i, group), inner]

    def plane_send(i):
        r = plane_ref(i, g)
        return remote(r, r, x_send.at[i], x_recv.at[i], partner)

    def rim_send(e, group):
        r = w.at[group, pl.ds(half * group, half), edges[e]]
        return remote(r, r, x_send.at[4 + e], x_recv.at[4 + e], partner)

    arrive(0, 1)
    for _, _, c in halos[first_count:]:
        c.start()

    @pl.loop(0, LX + 2)
    def _(k):
        @pl.when(k == 1)
        def _():
            arrive(1, u_count)
            arrive(first_count, len(halos))

            @pl.loop(0, (LX + 2) // 2)
            def _(x):
                for i in range(2):
                    u1[2 * x + i] = u_step(ue, 2 * x + i + 1)

        @pl.when(k == 4)
        def _():
            arrive(u_count, u_count + 2)

        x = jnp.where(k < 4, 2 + k, jnp.where(k < 6, 5 - k, k))
        first_rows(jnp.where(g == 0, x, LX + 1 - x), range(2, LY))

        @pl.when(k >= 2)
        def _():
            second_rows(plane_of(k - 2, g), range(2, LY - 2))

        @pl.when(jnp.logical_and(k >= 2, k < 6))
        def _():
            plane_send(k - 2).start()

    arrive(u_count + 2, first_count)

    @pl.loop(0, (LX + 2) // 2)
    def _(x):
        for i in range(2):
            first_rows(2 * x + i, (0, 1, LY, LY + 1))

    @pl.loop(0, half)
    def _(h):
        for i in range(2):
            x = 2 * h + i
            x = jnp.where(g == 0, x, LX - 1 - x)
            second_rows(x, (0, 1, LY - 2, LY - 1))

        @pl.when(h == 1)
        def _():
            for e in range(2):
                rim_send(e, g).start()

    def tail(i):
        lo, n = TAIL[i]
        r = w.at[0, pl.ds(lo, n)]
        return remote(r, r, x_send.at[6 + i], x_recv.at[6 + i], (1, gx, gy))

    def tail_start(i):
        @pl.when(g == 0)
        def _():
            tail(i).start()

    tail_start(0)

    @pl.loop(0, LX // 2)
    def _(x):
        for i in range(2):
            c = u_step(u1, 2 * x + i + 1)[8:24]
            base_out[2 * x + i] = jnp.where(g == 0, c[:, :HALF], c[:, HALF:])

    def gram_rows(a, b, x, lo, n, acc, unroll):
        def step(y, acc):
            r = w[a, x, y]
            return tuple(acc[j] + r * w[b, x, y, pl.ds(j, 1), :] for j in range(NF))

        return lax.fori_loop(lo, lo + n, step, acc, unroll=unroll)

    zeros = tuple(jnp.zeros((NF, NZ), F32) for _ in range(NF))
    own = lax.fori_loop(0, LX, lambda x, acc: gram_rows(g, g, x, 0, LY, acc, 4), zeros)
    col = lax.broadcasted_iota(jnp.int32, (NF, 128), 1)
    part = jnp.zeros((NF, 128), F32)
    for j in range(NF):
        part = jnp.where(col == 8 + 8 * g + j, jnp.sum(own[j], axis=1, keepdims=True), part)
    cross = zeros
    for i in range(4):
        plane_send(i).wait_recv()
        cross = gram_rows(1, 0, plane_of(i, other), 2, LY - 4, cross, 4)
    for e in range(2):
        rim_send(e, other).wait_recv()

    def rim_gram(x, acc):
        acc = gram_rows(1, 0, half * other + x, 0, 2, acc, 2)
        return gram_rows(1, 0, half * other + x, LY - 2, 2, acc, 2)

    cross = lax.fori_loop(0, half, rim_gram, cross)
    for j in range(NF):
        part = jnp.where(col == j, jnp.sum(cross[j], axis=1, keepdims=True), part)
    me = g * GY + gy
    sub8 = lax.broadcasted_iota(jnp.int32, (NF, 128), 0)
    quarter = sub8 & 3
    wide = jnp.where(quarter == 0, part, 0.0)
    for k in range(1, 4):
        wide = jnp.where(quarter == k, pltpu.roll(part, 32 * k, 1), wide)
    part = jnp.concatenate(
        [jnp.sum(wide[4 * r : 4 * r + 4], axis=0, keepdims=True) for r in range(2)], axis=0
    )
    tile[0] = part
    al[me] = part

    def p_copy(i):
        off, swap = P_ORDER[i]
        dev = (other if swap else g, gx, lax.rem(gy + off, GY))
        return remote(tile.at[0], al.at[me], p_send.at[i], p_recv.at[me], dev)

    for i in range(len(P_ORDER)):
        p_copy(i).start()

    def z_copy(off):
        dev = (g, lax.rem(gx + off, GX), gy)
        return remote(tile.at[1], zl.at[gx], z_send.at[off], z_recv.at[gx], dev)

    tail_start(1)
    for s in range(2 * GY):
        c = remote(tile.at[0], al.at[s], p_send.at[0], p_recv.at[s], partner)
        when(me != s, c.wait_recv)
    total = al[0]
    for s in range(1, 2 * GY):
        total = total + al[s]
    tile[1] = total
    zl[gx] = total
    for off in Z_ORDER:
        z_copy(off).start()
    tail_start(2)
    for to, _, c in halos:
        when(to, c.wait_send)
    for i in range(4):
        plane_send(i).wait_send()
    for e in range(2):
        rim_send(e, g).wait_send()
    for i in range(len(P_ORDER)):
        p_copy(i).wait_send()
    for s in range(GX):
        c = remote(tile.at[1], zl.at[s], z_send.at[0], z_recv.at[s], partner)
        when(gx != s, c.wait_recv)
    total = zl[0]
    for s in range(1, GX):
        total = total + zl[s]

    total = total * (1.0 / CELLS)
    wide = jnp.where(sub8 < 4, total[0:1], total[1:2])
    gram = wide
    for k in range(1, 4):
        gram = jnp.where(quarter == k, pltpu.roll(wide, 128 - 32 * k, 1), gram)
    g01 = jnp.zeros((NF, 128), F32)
    for j in range(NF):
        row = jnp.where(col == sub8, gram[j : j + 1, :], 0.0)
        g01 = jnp.where(col == 8 + j, jnp.sum(row, axis=1, keepdims=True), g01)
    shifted = pltpu.roll(gram, 120, 1)
    top = jnp.where(col < 8, shifted, g01)
    low = jnp.where(col < 8, gram, shifted)
    top = jnp.where(col < 16, top, jnp.where(col == 16 + sub8, 1.0, 0.0))
    low = jnp.where(col < 16, low, jnp.where(col == 24 + sub8, 1.0, 0.0))
    m = jnp.concatenate([top, low], axis=0)
    sub = lax.broadcasted_iota(jnp.int32, (2 * NF, 128), 0)
    col16 = lax.broadcasted_iota(jnp.int32, (2 * NF, 128), 1)
    spread = [jnp.broadcast_to(m[:, j : j + 1], m.shape) for j in range(2 * NF)]
    for k in range(2 * NF - 1):
        factor = jnp.where(sub > k, spread[k] / spread[k][k : k + 1, :], 0.0)
        for j in range(k + 1, 2 * NF):
            spread[j] = spread[j] - factor * spread[j][k : k + 1, :]
        m = m - factor * m[k : k + 1, :]
    diag = jnp.where(col16 == sub, m, 0.0)
    root_row = jnp.sqrt(jnp.sum(diag, axis=0, keepdims=True))
    root_col = jnp.sqrt(jnp.sum(diag, axis=1, keepdims=True))
    growth_out[...] = jnp.log(root_row)[:, :16]
    inv = m / root_col
    coef_out[...] = jnp.where(g == 0, inv[:NF], inv[NF:])

    @pl.when(g == 1)
    def _():
        for i in range(len(TAIL)):
            tail(i).wait_recv()

    for off in Z_ORDER:
        z_copy(off).wait_send()

    @pl.when(g == 0)
    def _():
        for i in range(len(TAIL)):
            tail(i).wait_send()


def apply_kernel(
    w, base, coef, growth, base_hbm, ortho_hbm, growth_hbm, o, out_sem
):
    g = lax.axis_index("grp")
    small = [
        pltpu.make_async_copy(base, base_hbm, out_sem.at[PARTS * NF]),
        pltpu.make_async_copy(growth, growth_hbm, out_sem.at[PARTS * NF + 1]),
    ]
    for c in small:
        c.start()
    step = LX // PARTS

    def out_copy(q, f):
        r = pl.ds(q * step, step)
        return pltpu.make_async_copy(
            o.at[r, :, f], ortho_hbm.at[f, r], out_sem.at[q * NF + f]
        )

    def emit(groups):
        cols = [
            jnp.broadcast_to(coef[:, 16 + j : 17 + j], (NF, NZ)) for j in range(NF * groups)
        ]

        def plane(x, carry):
            def row(y, carry):
                acc = None
                for b in range(groups):
                    for j in range(NF):
                        t = cols[b * NF + j] * w[b, x, y, pl.ds(j, 1), :]
                        acc = t if acc is None else acc + t
                o[x, y] = acc
                return carry

            return lax.fori_loop(0, LY, row, carry, unroll=8)

        for q in range(PARTS):
            lax.fori_loop(q * step, (q + 1) * step, plane, 0)
            for f in range(NF):
                out_copy(q, f).start()

    @pl.when(g == 0)
    def _():
        emit(1)

    @pl.when(g == 1)
    def _():
        emit(2)

    for q in range(PARTS):
        for f in range(NF):
            out_copy(q, f).wait()
    for c in small:
        c.wait()


def body(*arrays):
    base_flow, fields = arrays[:2]
    vmem = pl.BlockSpec(memory_space=pltpu.VMEM)
    hbm = pl.BlockSpec(memory_space=pltpu.HBM)
    dma = pltpu.SemaphoreType.DMA
    stepped, base, coef, growth = pl.pallas_call(
        kernel,
        out_shape=[
            pltpu.VMEM((2, LX, LY, NF, NZ), F32),
            pltpu.VMEM(base_flow.shape, F32),
            pltpu.VMEM((NF, 128), F32),
            pltpu.VMEM((1, 2 * NF), F32),
        ],
        in_specs=[hbm] * 4,
        out_specs=[vmem] * 4,
        scratch_shapes=[
            pltpu.VMEM((LX + 4, LY + 4, NF, NZ), F32),
            pltpu.VMEM((LX + 2, LY + 2, NF, NZ), F32),
            pltpu.VMEM((LX + 4, 32, NZ), F32),
            pltpu.VMEM((LX + 2, 32, NZ), F32),
            pltpu.VMEM((2, LY, NZ), jnp.int32),
            pltpu.VMEM((2, 32, NZ), F32),
            pltpu.VMEM((2, 2, 128), F32),
            pltpu.VMEM((2 * GY, 2, 128), F32),
            pltpu.VMEM((GX, 2, 128), F32),
            dma((NF + 3,)),
            dma((32,)),
            dma((32,)),
            dma((9,)),
            dma((9,)),
            dma((2 * GY,)),
            dma((2 * GY,)),
            dma((GX,)),
            dma((GX,)),
        ],
        compiler_params=pltpu.CompilerParams(
            collective_id=0, has_side_effects=True, vmem_limit_bytes=16 << 20
        ),
    )(*(pltpu.with_memory_space_constraint(a, pltpu.HBM) for a in arrays))
    base, ortho, growth = pl.pallas_call(
        apply_kernel,
        out_shape=[
            jax.ShapeDtypeStruct(base_flow.shape, F32),
            jax.ShapeDtypeStruct(fields.shape, F32),
            jax.ShapeDtypeStruct((1, 2 * NF), F32),
        ],
        in_specs=[vmem] * 4,
        out_specs=[hbm] * 3,
        scratch_shapes=[pltpu.VMEM((LX, LY, NF, NZ), F32), dma((PARTS * NF + 2,))],
        compiler_params=pltpu.CompilerParams(vmem_limit_bytes=16 << 20),
    )(stepped, base, coef, growth)
    return base, ortho, growth.reshape(2 * NF)


def solution(mesh):
    in_specs = (P("gx", "gy", "grp"), P("grp", "gx", "gy", None), P("gy", None), P("gy", None))
    out_specs = (P("gx", "gy", "grp"), P("grp", "gx", "gy", None), P())
    return jax.shard_map(body, mesh=mesh, in_specs=in_specs, out_specs=out_specs, check_vma=False)
```
